256 devices in a mesh: ch: 8 (over y, core), seq: 32 (over x, z).
Axes of the slice: x: 4, y: 4, z: 8, core: 2. Of those that a mesh axis runs over, the one named last changes fastest.
Arguments:
- tokens: bfloat16 [24576, 4096], P('seq'), may hold values from -6 to 6
- in_weight: bfloat16 [4096, 3, 4096], P('seq', None, 'ch'), may hold values from -0.09375 to 0.09375
- short_weight: float32 [3, 3, 4096], P(None, None, 'ch'), may hold values from -3 to 3
- decay_rate: float32 [16, 4096], P(None, 'ch'), may hold values from 0 to 1
- residue: float32 [16, 4096], P(None, 'ch'), may hold values from -1.5 to 1.5
- out_weight: bfloat16 [4096, 4096], P('ch'), may hold values from -0.125 to 0.125
- contig_lengths: int32 [16], replicated, may hold values from 1 to 6144, 24576 in all
Outputs:
- mixed: bfloat16 [24576, 4096], P('seq', 'ch')
The draws below stay inside these ranges and needn't reach their ends.
Inputs may be any that keep to these rules, and one draw needn't show every extreme that they name: `contig_lengths`: the lengths sum to 24576; the largest is exactly 6144.
All inputs are finite; a program needn't handle non-finite values.
Results may differ from the reference program's by a relative error of at most 0.0049.
Values may be sent and summed in bfloat16 or wider, within the bound.
No kernel may reach another device: no remote copies, remote signals or barrier semaphores. Data moves between devices by JAX's collectives and lax.ppermute only.
A program may use at most 128 MiB of HBM per device.

```python
import math
import jax
import jax.numpy as jnp
import numpy as np
from jax import lax

D = 4096
MODES = 16
TOKENS = 24576
CONTIGS = 16
MOST = 6144


def draw_decay_rate(key, part):
    key = jax.random.fold_in(key, 7)
    pick_key, fast_key, slow_key = jax.random.split(key, 3)
    share = 0.5
    fast_log = jax.random.uniform(fast_key, (MODES, D), jnp.float32, jnp.log(1.0 / 50.0), jnp.log(1.0 / 30.0))
    slow_log = jax.random.uniform(slow_key, (MODES, D), jnp.float32, jnp.log(0.2 / TOKENS), jnp.log(2.3 / TOKENS))
    chosen = jax.random.bernoulli(pick_key, share, (MODES, D))
    return jnp.exp(jnp.where(chosen, fast_log, slow_log)).astype(jnp.float32)


def with_spikes(entries, own_key, source, target, parts, factor):
    def block_of(axis_at):
        return (jnp.arange(entries.shape[axis_at]) // (entries.shape[axis_at] // parts)).reshape((-1,) + (1,) * (entries.ndim - 1 - axis_at))

    one_side = jax.random.permutation(own_key, parts)[block_of(target)]
    far = (block_of(target) + parts // 2) % parts
    return jnp.where((block_of(source) == one_side) | (block_of(source) == far), factor * entries, entries)


def steps_of(key, dims, shards, least, high):
    level, own = 1.0, jax.random.fold_in(key, 6)
    for axis_at, blocks in shards:
        draws = jnp.exp(jax.random.uniform(jax.random.fold_in(own, axis_at), (blocks,), jnp.float32, least / len(shards), high / len(shards)))
        level = level * jnp.repeat(draws, dims[axis_at] // blocks).reshape([-1 if axis == axis_at else 1 for axis in range(len(dims))])
    return level


def profile(amount, total, most, slope):
    loads = [(1 << 20) // math.isqrt(standing ** slope) + 1 for standing in range(2, amount + 1)]
    spare, counts = total - most - (amount - 1), [1] * (amount - 1)
    while spare > 0:
        candidates = [i for i in range(amount - 1) if counts[i] < most]
        pool, left = sum([loads[i] for i in candidates]), spare
        for i in candidates:
            addition = min(most - counts[i], max(1, left * loads[i] // pool), spare)
            counts[i] = counts[i] + addition
            spare = spare - addition
    return np.array([most] + counts)


def uneven(stream_key, number_of, total, limit, lean):
    if number_of == 2:
        one = jax.random.randint(stream_key, (), max(1, total - limit), min(limit, total - 1) + 1)
        return jnp.stack([one, total - one])
    tallies = jnp.asarray(profile(number_of, total, limit, lean), jnp.int32)
    couples = (number_of - 1) // 2
    giver, sink = tallies[1:1 + 2 * couples:2], tallies[2:2 + 2 * couples:2]
    slack = jnp.minimum(giver - 1, limit - sink)
    shifted = jax.random.randint(jax.random.fold_in(stream_key, 1), (couples,), 0, 1 << 20) % (slack + 1)
    tallies = tallies.at[1:1 + 2 * couples:2].set(giver - shifted).at[2:2 + 2 * couples:2].set(sink + shifted)
    return tallies[jax.random.permutation(jax.random.fold_in(stream_key, 2), number_of)]


def gaussian(stream_key, shape, width, limit, cuts=(), kind=jnp.bfloat16):
    array = jax.random.normal(stream_key, shape, jnp.float32) * width
    if len(cuts) > 0:
        array = steps_of(stream_key, shape, cuts, -0.22, 0.18) * array
    return jnp.clip(array, min=-limit, max=limit).astype(kind)


def bell_draw_with(key, dims, deviation, most, cuts, heavy, kind=jnp.bfloat16):
    array = deviation * jax.random.normal(key, dims, jnp.float32)
    if cuts:
        array = array * steps_of(key, dims, cuts, -0.22, 0.18)
    return jnp.clip(with_spikes(array, jax.random.fold_in(key, 3), *heavy), -most, most).astype(kind)


def setup_inputs(seed: int = 0) -> dict:
    key_of = jax.random.split(jax.random.key(seed), 8)
    tokens = gaussian(key_of[0], (TOKENS, D), 1.0, 6.0, ((0, 32),))
    in_weight = gaussian(key_of[1], (D, 3, D), D ** -0.5, 0.09375, ((0, 32), (2, 8)))
    short_weight = gaussian(key_of[2], (3, 3, D), 0.6, 3.0, ((2, 8),), jnp.float32)
    decay_rate = draw_decay_rate(jax.random.fold_in(key_of[7], 71), 0)
    residue = gaussian(key_of[4], (MODES, D), 0.25, 1.5, ((1, 8),), jnp.float32)
    out_weight = bell_draw_with(key_of[5], (D, D), D ** -0.5, 0.125, ((0, 8),), (0, 1, 8, 2.0))
    contig_lengths = uneven(key_of[6], CONTIGS, TOKENS, MOST, 2).astype(jnp.int32)
    return {"tokens": tokens, "in_weight": in_weight, "short_weight": short_weight, "decay_rate": decay_rate, "residue": residue, "out_weight": out_weight, "contig_lengths": contig_lengths}


def reference(tokens, in_weight, short_weight, decay_rate, residue, out_weight, contig_lengths):
    projected = jnp.dot(tokens, in_weight.reshape(D, 3 * D), preferred_element_type=jnp.float32).reshape(TOKENS, 3, D)
    starts = (jnp.cumsum(contig_lengths) - contig_lengths).astype(jnp.int32)
    position = jnp.arange(TOKENS, dtype=jnp.int32)
    first_flag = jnp.any(position[:, None] == starts[None, :], axis=1).astype(jnp.int32)
    keep_flag = (1 - first_flag).astype(jnp.float32)
    keep_prev = jnp.concatenate([jnp.zeros((1,), jnp.float32), keep_flag[:-1]])
    mask_one = keep_flag
    mask_two = keep_flag * keep_prev
    prev_one = jnp.concatenate([jnp.zeros((1, 3, D), jnp.float32), projected[:-1]], axis=0)
    prev_two = jnp.concatenate([jnp.zeros((2, 3, D), jnp.float32), projected[:-2]], axis=0)
    filtered = short_weight[:, 0][None] * projected + mask_one[:, None, None] * (short_weight[:, 1][None] * prev_one) + mask_two[:, None, None] * (short_weight[:, 2][None] * prev_two)
    drive_in = filtered[:, 1] * filtered[:, 2]
    decay_step = jnp.exp(-decay_rate)
    coef_mode = residue * jnp.sqrt(-jnp.expm1(-2.0 * decay_rate))

    def advance(state_now, inputs):
        drive_row, keep_row = inputs
        state_now = decay_step * keep_row * state_now + drive_row[None, :]
        return (state_now, lax.optimization_barrier(jnp.sum(coef_mode * state_now, axis=0)))
    _, longconv = lax.scan(advance, jnp.zeros((MODES, D), jnp.float32), (drive_in, keep_flag))
    gated = (filtered[:, 0] * longconv).astype(jnp.bfloat16)
    return jnp.dot(gated, out_weight, preferred_element_type=jnp.float32).astype(jnp.bfloat16)
```

```python
import functools
import jax
import jax.numpy as jnp
from jax import lax
from jax.experimental import pallas as pl
from jax.experimental.pallas import tpu as pltpu
from jax.sharding import PartitionSpec as P

F32, BF16 = jnp.float32, jnp.bfloat16
HALO = 16
CHUNKS = 8
LANES = 128


def load_tokens(order, place_ref, tok_hbm, halo_hbm, tok, sem):
    rows = tok_hbm.shape[0]
    copies = [pltpu.make_async_copy(halo_hbm, tok.at[pl.ds(0, HALO)], sem)]
    body = tok.at[pl.ds(HALO, rows)]
    copies.append(pltpu.make_async_copy(tok_hbm, body, sem))
    for c in copies:
        c.start()
    for c in copies:
        c.wait()


def project(tok, pieces, acc, step=1024):
    first = True
    k0 = 0
    for w in pieces:
        depth = w.shape[0]
        size = min(step, depth)
        n = depth // size

        def one(i, k0=k0, w=w, size=size):
            at = pl.multiple_of(k0 + i * size, 128)
            wi = pl.multiple_of(i * size, 128)
            return jnp.dot(tok[:, pl.ds(at, size)], w[pl.ds(wi, size), :], preferred_element_type=F32)

        start = 0
        if first:
            acc[...] = one(0)
            first, start = False, 1

        @pl.loop(start, n)
        def _(i):
            acc[...] += one(i)

        k0 += depth


def short_filter(acc, cols, taps, keep, mask2, r0, rows):
    window = acc[pl.ds(pl.multiple_of(HALO - 8 + r0, 8), rows + 8), cols]
    cur, one, two = window[8:], window[7:-1], window[6:-2]
    return taps[0:1] * cur + keep * (taps[1:2] * one) + mask2 * (taps[2:3] * two)


def drive_kernel(order, block, place_ref, tok_hbm, halo_hbm, *refs):
    n = len(order)
    pieces, refs = refs[:n], refs[n:]
    kw, vw, keep_ref, mask2_ref, tail_ref, thru_ref, d_ref, dchunk_ref = refs[:8]
    u_ref, end_ref, last_ref, tok, acc, sem, drive, ends = refs[8:]

    @pl.when(pl.program_id(0) == 0)
    def _():
        load_tokens(order, place_ref, tok_hbm, halo_hbm, tok, sem)

    project(tok, pieces, acc)
    steps = u_ref.shape[1]
    modes = d_ref.shape[0]
    for s in range(block // LANES):
        kc = pl.ds(s * LANES, LANES)
        vc = pl.ds(block + s * LANES, LANES)

        @pl.loop(0, CHUNKS)
        def _(j):
            r0 = pl.multiple_of(j * steps, 8)
            keep, mask2 = keep_ref[pl.ds(r0, steps), :], mask2_ref[pl.ds(r0, steps), :]
            fk = short_filter(acc, kc, kw[:, kc], keep, mask2, r0, steps)
            fv = short_filter(acc, vc, vw[:, kc], keep, mask2, r0, steps)
            drive[pl.ds(r0, steps), :] = fk * fv

        d = [jnp.broadcast_to(d_ref[pl.ds(m, 1), kc], (CHUNKS, LANES)) for m in range(modes)]

        def step(t, state):
            u = drive[pl.ds(t, CHUNKS, stride=steps), :]
            u_ref[s, t] = u
            u = u * tail_ref[t]
            return tuple(d[m] * state[m] + u for m in range(modes))

        zero = jnp.zeros((CHUNKS, LANES), F32)
        state = lax.fori_loop(0, steps, step, (zero,) * modes, unroll=4)
        for m in range(modes):
            ends[m] = state[m]
        dc = dchunk_ref[:, kc]
        enter = jnp.zeros((modes, LANES), F32)
        for j in range(CHUNKS):
            mine = ends[:, j, :]
            end_ref[:, j, kc] = mine
            enter = dc * (enter * thru_ref[pl.ds(j, 1), :]) + mine
        last_ref[:, kc] = enter


def query_kernel(order, block, place_ref, tok_hbm, halo_hbm, *refs):
    n = len(order)
    pieces, refs = refs[:n], refs[n:]
    qw, keep_ref, mask2_ref, fq_ref, tok, acc, sem = refs

    @pl.when(pl.program_id(0) == 0)
    def _():
        load_tokens(order, place_ref, tok_hbm, halo_hbm, tok, sem)

    project(tok, pieces, acc)
    rows = fq_ref.shape[0]
    steps = rows // CHUNKS
    for s in range(block // LANES):
        c = pl.ds(s * LANES, LANES)

        @pl.loop(0, CHUNKS)
        def _(j):
            r0 = pl.multiple_of(j * steps, 8)
            keep, mask2 = keep_ref[pl.ds(r0, steps), :], mask2_ref[pl.ds(r0, steps), :]
            fq_ref[pl.ds(r0, steps), c] = short_filter(acc, c, qw[:, c], keep, mask2, r0, steps)


def gate_kernel(u_ref, end_ref, enter_ref, fq_ref, keep_ref, thru_ref, d_ref, dchunk_ref, coef_ref, out_ref, states, long):
    rows, block = fq_ref.shape
    steps = rows // CHUNKS
    modes = d_ref.shape[0]
    for s in range(block // LANES):
        c = pl.ds(s * LANES, LANES)
        dc = dchunk_ref[:, c]
        enter = enter_ref[:, c]
        for j in range(CHUNKS):
            states[:, j, :] = enter
            enter = dc * (enter * thru_ref[pl.ds(j, 1), :]) + end_ref[:, j, c]
        d = [jnp.broadcast_to(d_ref[pl.ds(m, 1), c], (CHUNKS, LANES)) for m in range(modes)]
        coef = [jnp.broadcast_to(coef_ref[pl.ds(m, 1), c], (CHUNKS, LANES)) for m in range(modes)]

        def step(t, state):
            at = pl.ds(t, CHUNKS, stride=steps)
            u, keep = u_ref[s, t], keep_ref[t]
            state = tuple(d[m] * (keep * state[m]) + u for m in range(modes))
            terms = [coef[m] * state[m] for m in range(modes)]
            while len(terms) > 1:
                terms = [a + b for a, b in zip(terms[::2], terms[1::2])]
            long[at, :] = terms[0]
            return state

        lax.fori_loop(0, steps, step, tuple(states[m] for m in range(modes)), unroll=2)

        @pl.loop(0, CHUNKS)
        def _(j):
            at = pl.ds(pl.multiple_of(j * steps, 16), steps)
            out_ref[at, c] = (fq_ref[at, c] * long[at, :]).astype(BF16)


def call_drive(place, tokens, halo, pieces, kw, vw, keep, mask2, tail, thru, d, dchunk, order, block):
    rows, width = tokens.shape
    modes, chans = d.shape
    grid = chans // block
    anywhere = pl.BlockSpec(memory_space=pl.ANY)
    fixed = lambda a: pl.BlockSpec(a.shape, lambda b: (0,) * a.ndim)
    per_chan = lambda a: pl.BlockSpec((a.shape[0], block), lambda b: (0, b))
    return pl.pallas_call(
        functools.partial(drive_kernel, order, block),
        grid=(grid,),
        out_shape=[
            jax.ShapeDtypeStruct((chans // LANES, rows // CHUNKS, CHUNKS, LANES), F32),
            jax.ShapeDtypeStruct((modes, CHUNKS, chans), F32),
            jax.ShapeDtypeStruct((modes, chans), F32),
        ],
        in_specs=[pl.BlockSpec(memory_space=pltpu.SMEM), anywhere, anywhere]
        + [pl.BlockSpec((w.shape[0], 2 * block), lambda b: (0, b)) for w in pieces]
        + [per_chan(kw), per_chan(vw), fixed(keep), fixed(mask2), fixed(tail), fixed(thru), per_chan(d), per_chan(dchunk)],
        out_specs=[
            pl.BlockSpec((block // LANES, rows // CHUNKS, CHUNKS, LANES), lambda b: (b, 0, 0, 0)),
            pl.BlockSpec((modes, CHUNKS, block), lambda b: (0, 0, b)),
            pl.BlockSpec((modes, block), lambda b: (0, b)),
        ],
        scratch_shapes=[
            pltpu.VMEM((HALO + rows, width), BF16),
            pltpu.VMEM((HALO + rows, 2 * block), F32),
            pltpu.SemaphoreType.DMA,
            pltpu.VMEM((rows, LANES), F32),
            pltpu.VMEM((modes, CHUNKS, LANES), F32),
        ],
        compiler_params=pltpu.CompilerParams(vmem_limit_bytes=48 * 2**20),
        cost_estimate=pl.CostEstimate(flops=4 * rows * width * chans, bytes_accessed=2 * width * (rows + 2 * chans), transcendentals=0),
        name="drive",
    )(place, tokens, halo, *pieces, kw, vw, keep, mask2, tail, thru, d, dchunk)


def call_query(place, tokens, halo, pieces, qw, keep, mask2, order, block, first=0):
    rows, width = tokens.shape
    chans = qw.shape[1]
    grid = chans // block
    anywhere = pl.BlockSpec(memory_space=pl.ANY)
    fixed = lambda a: pl.BlockSpec(a.shape, lambda b: (0,) * a.ndim)
    return pl.pallas_call(
        functools.partial(query_kernel, order, block),
        grid=(grid,),
        out_shape=jax.ShapeDtypeStruct((rows, chans), F32),
        in_specs=[pl.BlockSpec(memory_space=pltpu.SMEM), anywhere, anywhere]
        + [pl.BlockSpec((w.shape[0], block), lambda b: (0, first + b)) for w in pieces]
        + [pl.BlockSpec((qw.shape[0], block), lambda b: (0, b)), fixed(keep), fixed(mask2)],
        out_specs=pl.BlockSpec((rows, block), lambda b: (0, b)),
        scratch_shapes=[
            pltpu.VMEM((HALO + rows, width), BF16),
            pltpu.VMEM((HALO + rows, block), F32),
            pltpu.SemaphoreType.DMA,
        ],
        compiler_params=pltpu.CompilerParams(vmem_limit_bytes=48 * 2**20),
        cost_estimate=pl.CostEstimate(flops=2 * rows * width * chans, bytes_accessed=2 * width * (rows + chans), transcendentals=0),
        name="query",
    )(place, tokens, halo, *pieces, qw, keep, mask2)


def call_gate(u, ends, enter, fq, keep, thru, d, dchunk, coef, block):
    rows, chans = fq.shape
    modes = d.shape[0]
    fixed = lambda a: pl.BlockSpec(a.shape, lambda b: (0,) * a.ndim)
    per_chan = lambda a: pl.BlockSpec((a.shape[0], block), lambda b: (0, b))
    return pl.pallas_call(
        gate_kernel,
        grid=(chans // block,),
        out_shape=jax.ShapeDtypeStruct((rows, chans), BF16),
        in_specs=[
            pl.BlockSpec((block // LANES, rows // CHUNKS, CHUNKS, LANES), lambda b: (b, 0, 0, 0)),
            pl.BlockSpec((modes, CHUNKS, block), lambda b: (0, 0, b)),
            per_chan(enter), per_chan(fq), fixed(keep), fixed(thru), per_chan(d), per_chan(dchunk), per_chan(coef),
        ],
        out_specs=pl.BlockSpec((rows, block), lambda b: (0, b)),
        scratch_shapes=[pltpu.VMEM((modes, CHUNKS, LANES), F32), pltpu.VMEM((rows, LANES), F32)],
        compiler_params=pltpu.CompilerParams(vmem_limit_bytes=32 * 2**20),
        cost_estimate=pl.CostEstimate(flops=5 * rows * modes * chans, bytes_accessed=10 * rows * chans, transcendentals=0),
        name="gate",
    )(u, ends, enter, fq, keep, thru, d, dchunk, coef)


def flags(contig_lengths, shard_at, rows):
    starts = jnp.cumsum(contig_lengths) - contig_lengths
    base = shard_at * rows
    position = base - 1 + jnp.arange(rows + 1, dtype=jnp.int32)
    first = jnp.any(position[:, None] == starts[None, :], axis=1)
    keep_ext = jnp.where(first, 0.0, 1.0).astype(F32)
    keep = keep_ext[1:]
    mask2 = keep * keep_ext[:-1]
    steps = rows // CHUNKS
    here = position[1:, None]
    chunk_end = base + (jnp.arange(rows, dtype=jnp.int32)[:, None] // steps + 1) * steps
    tail = jnp.where(jnp.any((starts[None] > here) & (starts[None] < chunk_end), axis=1), 0.0, 1.0).astype(F32)
    lo = base + jnp.arange(CHUNKS, dtype=jnp.int32)[:, None] * steps
    thru = jnp.where(jnp.any((starts[None] >= lo) & (starts[None] < lo + steps), axis=1), 0.0, 1.0).astype(F32)
    wide = lambda a: jnp.broadcast_to(a[:, None], (a.shape[0], LANES))
    slots = lambda a: wide(a).reshape(CHUNKS, steps, LANES).transpose(1, 0, 2)
    return starts, wide(keep), wide(mask2), slots(keep), slots(tail), wide(thru)


def send(value, axis, pairs):
    return lax.ppermute(value, axis, pairs)


def shift_up(size, distance):
    return [(i, i + distance) for i in range(size - distance)]


def swap_cores(size):
    return [(i, i ^ 1) for i in range(size)]


def entering_state(last, starts, decay_shard, shard_at, rows, shards, most):
    state = send(last, "seq", shift_up(shards, 1))
    window = 1
    while window * rows < most:
        lo = (shard_at - window) * rows
        thru = jnp.where(jnp.any((starts >= lo) & (starts < shard_at * rows)), 0.0, 1.0)
        state = state + (thru * decay_shard**window) * send(state, "seq", shift_up(shards, window))
        window *= 2
    return state


def sum_over_channels(gated, out_weight, chips, y, core):
    rows = gated.shape[0]
    width = out_weight.shape[1] // (2 * chips)
    way = 1 - 2 * core
    ring = [(2 * i + c, 2 * ((i + 1 - 2 * c) % chips) + c) for i in range(chips) for c in range(2)]
    partials = []
    for k in range(chips - 1, -1, -1):
        mine_at = (2 * ((y + k * way) % chips) + core) * width
        other_at = (2 * ((y - k * way) % chips) + 1 - core) * width
        columns = lambda at: lax.dynamic_slice_in_dim(out_weight, at, width, axis=1)
        other = jnp.dot(gated, columns(other_at), preferred_element_type=F32).astype(BF16)
        partials.append((columns(mine_at), send(other, "ch", swap_cores(2 * chips))))
    total = None
    for mine, other in partials:
        block = jnp.dot(gated, mine, preferred_element_type=F32) + other.astype(F32)
        if total is not None:
            block = block + send(total, "ch", ring).astype(F32)
        total = block.astype(BF16)
    return total


def per_device(tokens, in_weight, short_weight, decay_rate, residue, out_weight, contig_lengths):
    rows, width = tokens.shape
    chans = in_weight.shape[2]
    shards, chips = lax.axis_size("seq"), lax.axis_size("ch") // 2
    shard_at, place_ch = lax.axis_index("seq"), lax.axis_index("ch")
    y, core = place_ch // 2, place_ch % 2
    block = 2 * LANES
    most = 6144

    halo = send(tokens[rows - HALO :], "seq", shift_up(shards, 1))
    grouped = in_weight.reshape(-1, 3, chans // block, block)
    kv = jnp.concatenate([grouped[:, 1], grouped[:, 2]], axis=2).reshape(-1, 2 * chans)
    own = jnp.concatenate([kv, in_weight[:, 0]], axis=1)
    whole = lax.all_gather(own, "seq", axis=0, tiled=True)

    starts, keep, mask2, keep_s, tail, thru = flags(contig_lengths, shard_at, rows)
    coef = residue * jnp.sqrt(-jnp.expm1(-2.0 * decay_rate))
    d = jnp.exp(-decay_rate)
    d_chunk = jnp.exp(-decay_rate * (rows // CHUNKS))
    d_shard = jnp.exp(-decay_rate * rows)
    place = jnp.zeros((2,), jnp.int32)
    kw, vw, qw = short_weight[1], short_weight[2], short_weight[0]
    drive, ends, last = call_drive(place, tokens, halo, [whole], kw, vw, keep, mask2, tail, thru, d, d_chunk, [0], block)
    enter = entering_state(last, starts, d_shard, shard_at, rows, shards, most)
    fq = call_query(place, tokens, halo, [whole], qw, keep, mask2, [0], block, 2 * chans // block)
    gated = call_gate(drive, ends, enter, fq, keep_s, thru, d, d_chunk, coef, block)
    return sum_over_channels(gated, out_weight, chips, y, core)


def solution(mesh):
    placed = (
        P("seq", None),
        P("seq", None, "ch"),
        P(None, None, "ch"),
        P(None, "ch"),
        P(None, "ch"),
        P("ch", None),
        P(),
    )
    return jax.shard_map(
        per_device, mesh=mesh, in_specs=placed, out_specs=P("seq", "ch"), check_vma=False
    )
```

```python
import functools
import jax
import jax.numpy as jnp
from jax import lax
from jax.experimental import pallas as pl
from jax.experimental.pallas import tpu as pltpu
from jax.sharding import PartitionSpec as P

F32, BF16 = jnp.float32, jnp.bfloat16
HALO = 16
CHUNKS = 8
LANES = 128


def tokens_copies(tok_hbm, halo_hbm, tok, sem):
    rows = tok_hbm.shape[0]
    return [
        pltpu.make_async_copy(halo_hbm, tok.at[pl.ds(0, HALO)], sem),
        pltpu.make_async_copy(tok_hbm, tok.at[pl.ds(HALO, rows)], sem),
    ]


def weight_copies(moves, place, sources, weight, depth, cols, sem):
    x, z, core = place[0], place[1], place[2]
    way = 1 - 2 * core
    copies = []
    for source, index, row, rows, dx, dz, half in moves:
        dx = jnp.where(core == 0, dx[0], dx[1]) if isinstance(dx, tuple) else dx
        at = (lax.rem(x + dx * way + 4, 4) * 8 + lax.rem(z + dz * way + 8, 8)) * depth
        if half is not None:
            at = at + (core if half == "own" else 1 - core) * rows
        ref = sources[source]
        for i in index:
            ref = ref.at[i]
        at = pl.multiple_of(at, 16)
        copies.append(
            pltpu.make_async_copy(ref.at[pl.ds(row, rows), cols], weight.at[pl.ds(at, rows)], sem)
        )
    return copies


def project(tok, weight, acc, step=1024):
    def one(i):
        at = pl.multiple_of(i * step, step)
        return jnp.dot(tok[:, pl.ds(at, step)], weight[pl.ds(at, step), :], preferred_element_type=F32)

    acc[...] = one(0)

    @pl.loop(1, weight.shape[0] // step)
    def _(i):
        acc[...] += one(i)


def short_filter(acc, cols, taps, keep, mask2, r0, rows):
    window = acc[pl.ds(pl.multiple_of(HALO - 8 + r0, 8), rows + 8), cols]
    cur, one, two = window[8:], window[7:-1], window[6:-2]
    return taps[0:1] * cur + keep * (taps[1:2] * one) + mask2 * (taps[2:3] * two)


def drive_kernel(moves, block, count, place, tok_hbm, halo_hbm, *refs):
    sources, refs = refs[:count], refs[count:]
    kw, vw, keep_ref, mask2_ref, tail_ref, thru_ref, d_ref, dchunk_ref = refs[:8]
    u_ref, end_ref, last_ref, tok, weights, acc, sem, wsem, drive, ends = refs[8:]
    depth = tok.shape[1] // 32
    steps = u_ref.shape[1]
    modes = d_ref.shape[0]
    blocks = weights.shape[0]

    def copies(b):
        return weight_copies(moves, place, sources, weights.at[b], depth, pl.ds(b * 2 * block, 2 * block), wsem.at[b])

    loads = tokens_copies(tok_hbm, halo_hbm, tok, sem)
    fetch = [copies(b) for b in range(blocks)]
    for c in loads + sum(fetch, []):
        c.start()
    for c in loads:
        c.wait()
    for b in range(blocks):
        for c in fetch[b]:
            c.wait()
        project(tok, weights.at[b], acc)
        for s in range(block // LANES):
            g = b * (block // LANES) + s
            at = pl.ds(g * LANES, LANES)
            kc = pl.ds(s * LANES, LANES)
            vc = pl.ds(block + s * LANES, LANES)

            @pl.loop(0, CHUNKS)
            def _(j):
                r0 = pl.multiple_of(j * steps, 8)
                keep, mask2 = keep_ref[pl.ds(r0, steps), :], mask2_ref[pl.ds(r0, steps), :]
                fk = short_filter(acc, kc, kw[:, at], keep, mask2, r0, steps)
                fv = short_filter(acc, vc, vw[:, at], keep, mask2, r0, steps)
                drive[pl.ds(r0, steps), :] = fk * fv

            d = [jnp.broadcast_to(d_ref[pl.ds(m, 1), at], (CHUNKS, LANES)) for m in range(modes)]

            def step(t, state):
                u = drive[pl.ds(t, CHUNKS, stride=steps), :]
                u_ref[g, t] = u
                u = u * tail_ref[t]
                return tuple(d[m] * state[m] + u for m in range(modes))

            zero = jnp.zeros((CHUNKS, LANES), F32)
            state = lax.fori_loop(0, steps, step, (zero,) * modes, unroll=4)
            for m in range(modes):
                ends[m] = state[m]
            dc = dchunk_ref[:, at]
            enter = jnp.zeros((modes, LANES), F32)
            for j in range(CHUNKS):
                mine = ends[:, j, :]
                end_ref[:, j, at] = mine
                enter = dc * (enter * thru_ref[pl.ds(j, 1), :]) + mine
            last_ref[:, at] = enter


def query_kernel(moves, count, place, tok_hbm, halo_hbm, *refs):
    sources, refs = refs[:count], refs[count:]
    qw, keep_ref, mask2_ref, fq_ref, tok, weight, acc, sem, wsem = refs
    depth = tok.shape[1] // 32
    copies = tokens_copies(tok_hbm, halo_hbm, tok, sem)
    copies += weight_copies(moves, place, sources, weight, depth, slice(None), wsem)
    for c in copies:
        c.start()
    for c in copies:
        c.wait()
    project(tok, weight, acc)
    rows, chans = fq_ref.shape
    steps = rows // CHUNKS
    for s in range(chans // LANES):
        c = pl.ds(s * LANES, LANES)

        @pl.loop(0, CHUNKS)
        def _(j):
            r0 = pl.multiple_of(j * steps, 8)
            keep, mask2 = keep_ref[pl.ds(r0, steps), :], mask2_ref[pl.ds(r0, steps), :]
            fq_ref[pl.ds(r0, steps), c] = short_filter(acc, c, qw[:, c], keep, mask2, r0, steps)


def gate_kernel(u_ref, end_ref, enter_ref, fq_ref, keep_ref, thru_ref, d_ref, dchunk_ref, coef_ref, out_ref, states, long):
    rows, block = fq_ref.shape
    steps = rows // CHUNKS
    modes = d_ref.shape[0]
    for s in range(block // LANES):
        c = pl.ds(s * LANES, LANES)
        dc = dchunk_ref[:, c]
        enter = enter_ref[:, c]
        for j in range(CHUNKS):
            states[:, j, :] = enter
            enter = dc * (enter * thru_ref[pl.ds(j, 1), :]) + end_ref[:, j, c]
        d = [jnp.broadcast_to(d_ref[pl.ds(m, 1), c], (CHUNKS, LANES)) for m in range(modes)]
        coef = [jnp.broadcast_to(coef_ref[pl.ds(m, 1), c], (CHUNKS, LANES)) for m in range(modes)]

        def step(t, state):
            at = pl.ds(t, CHUNKS, stride=steps)
            u, keep = u_ref[s, t], keep_ref[t]
            state = tuple(d[m] * (keep * state[m]) + u for m in range(modes))
            terms = [coef[m] * state[m] for m in range(modes)]
            while len(terms) > 1:
                terms = [a + b for a, b in zip(terms[::2], terms[1::2])]
            long[at, :] = terms[0]
            return state

        lax.fori_loop(0, steps, step, tuple(states[m] for m in range(modes)), unroll=2)

        @pl.loop(0, CHUNKS)
        def _(j):
            at = pl.ds(pl.multiple_of(j * steps, 16), steps)
            out_ref[at, c] = (fq_ref[at, c] * long[at, :]).astype(BF16)


ANYWHERE = pl.BlockSpec(memory_space=pl.ANY)
IN_VMEM = pl.BlockSpec(memory_space=pltpu.VMEM)
IN_SMEM = pl.BlockSpec(memory_space=pltpu.SMEM)


def call_drive(place, tokens, halo, sources, moves, kw, vw, keep, mask2, tail, thru, d, dchunk, block):
    rows, width = tokens.shape
    modes, chans = d.shape
    blocks = chans // block
    return pl.pallas_call(
        functools.partial(drive_kernel, moves, block, len(sources)),
        out_shape=[
            jax.ShapeDtypeStruct((chans // LANES, rows // CHUNKS, CHUNKS, LANES), F32),
            jax.ShapeDtypeStruct((modes, CHUNKS, chans), F32),
            jax.ShapeDtypeStruct((modes, chans), F32),
        ],
        in_specs=[IN_SMEM, ANYWHERE, ANYWHERE] + [ANYWHERE] * len(sources) + [IN_VMEM] * 8,
        out_specs=[IN_VMEM] * 3,
        scratch_shapes=[
            pltpu.VMEM((HALO + rows, width), BF16),
            pltpu.VMEM((blocks, width, 2 * block), BF16),
            pltpu.VMEM((HALO + rows, 2 * block), F32),
            pltpu.SemaphoreType.DMA,
            pltpu.SemaphoreType.DMA((blocks,)),
            pltpu.VMEM((rows, LANES), F32),
            pltpu.VMEM((modes, CHUNKS, LANES), F32),
        ],
        compiler_params=pltpu.CompilerParams(vmem_limit_bytes=40 * 2**20),
        cost_estimate=pl.CostEstimate(flops=8 * rows * width * chans, bytes_accessed=2 * width * (rows + 2 * chans), transcendentals=0),
        name="drive",
    )(place, tokens, halo, *sources, kw, vw, keep, mask2, tail, thru, d, dchunk)


def call_query(place, tokens, halo, sources, moves, qw, keep, mask2):
    rows, width = tokens.shape
    chans = qw.shape[1]
    return pl.pallas_call(
        functools.partial(query_kernel, moves, len(sources)),
        out_shape=jax.ShapeDtypeStruct((rows, chans), F32),
        in_specs=[IN_SMEM, ANYWHERE, ANYWHERE] + [ANYWHERE] * len(sources) + [IN_VMEM] * 3,
        out_specs=IN_VMEM,
        scratch_shapes=[
            pltpu.VMEM((HALO + rows, width), BF16),
            pltpu.VMEM((width, chans), BF16),
            pltpu.VMEM((HALO + rows, chans), F32),
            pltpu.SemaphoreType.DMA,
            pltpu.SemaphoreType.DMA,
        ],
        compiler_params=pltpu.CompilerParams(vmem_limit_bytes=40 * 2**20),
        cost_estimate=pl.CostEstimate(flops=4 * rows * width * chans, bytes_accessed=2 * width * (rows + chans), transcendentals=0),
        name="query",
    )(place, tokens, halo, *sources, qw, keep, mask2)


def call_gate(u, ends, enter, fq, keep, thru, d, dchunk, coef, block):
    rows, chans = fq.shape
    modes = d.shape[0]
    fixed = lambda a: pl.BlockSpec(a.shape, lambda b: (0,) * a.ndim)
    per_chan = lambda a: pl.BlockSpec((a.shape[0], block), lambda b: (0, b))
    return pl.pallas_call(
        gate_kernel,
        grid=(chans // block,),
        out_shape=jax.ShapeDtypeStruct((rows, chans), BF16),
        in_specs=[
            pl.BlockSpec((block // LANES, rows // CHUNKS, CHUNKS, LANES), lambda b: (b, 0, 0, 0)),
            pl.BlockSpec((modes, CHUNKS, block), lambda b: (0, 0, b)),
            per_chan(enter), per_chan(fq), fixed(keep), fixed(thru), per_chan(d), per_chan(dchunk), per_chan(coef),
        ],
        out_specs=pl.BlockSpec((rows, block), lambda b: (0, b)),
        scratch_shapes=[pltpu.VMEM((modes, CHUNKS, LANES), F32), pltpu.VMEM((rows, LANES), F32)],
        compiler_params=pltpu.CompilerParams(vmem_limit_bytes=32 * 2**20),
        cost_estimate=pl.CostEstimate(flops=5 * rows * modes * chans, bytes_accessed=10 * rows * chans, transcendentals=0),
        name="gate",
    )(u, ends, enter, fq, keep, thru, d, dchunk, coef)


def flags(contig_lengths, shard_at, rows):
    starts = jnp.cumsum(contig_lengths) - contig_lengths
    base = shard_at * rows
    position = base - 1 + jnp.arange(rows + 1, dtype=jnp.int32)
    first = jnp.any(position[:, None] == starts[None, :], axis=1)
    keep_ext = jnp.where(first, 0.0, 1.0).astype(F32)
    keep = keep_ext[1:]
    mask2 = keep * keep_ext[:-1]
    steps = rows // CHUNKS
    here = position[1:, None]
    chunk_end = base + (jnp.arange(rows, dtype=jnp.int32)[:, None] // steps + 1) * steps
    tail = jnp.where(jnp.any((starts[None] > here) & (starts[None] < chunk_end), axis=1), 0.0, 1.0).astype(F32)
    lo = base + jnp.arange(CHUNKS, dtype=jnp.int32)[:, None] * steps
    thru = jnp.where(jnp.any((starts[None] >= lo) & (starts[None] < lo + steps), axis=1), 0.0, 1.0).astype(F32)
    wide = lambda a: jnp.broadcast_to(a[:, None], (a.shape[0], LANES))
    slots = lambda a: wide(a).reshape(CHUNKS, steps, LANES).transpose(1, 0, 2)
    return starts, wide(keep), wide(mask2), slots(keep), slots(tail), wide(thru)


def mix_kernel(place, own, theirs, near, far, mid_own, mid_other, w_mine, w_theirs, out_ref):
    core = place[2]
    half = out_ref.shape[0] // 2
    near_at = jnp.where(core == 0, 1, 3)
    far_at = 4 - near_at
    dot = functools.partial(jnp.dot, preferred_element_type=F32)

    @pl.loop(0, 2)
    def _(i):
        rows = pl.ds(pl.multiple_of(i * half, 16), half)
        total = dot(own[rows, :], w_mine[0]) + dot(theirs[rows, :], w_theirs[0])
        total += dot(near[0, rows, :], w_mine[near_at]) + dot(near[1, rows, :], w_theirs[near_at])
        total += dot(far[1, rows, :], w_mine[far_at]) + dot(far[0, rows, :], w_theirs[far_at])
        mine = jnp.where(i == core, mid_own[0], mid_other[1])
        other = jnp.where(i == core, mid_own[1], mid_other[0])
        total += dot(mine, w_mine[2]) + dot(other, w_theirs[2])
        out_ref[rows, :] = total.astype(BF16)


def call_mix(place, own, theirs, near, far, mid_own, mid_other, w_mine, w_theirs):
    rows, chans = own.shape
    width = w_mine.shape[2]
    return pl.pallas_call(
        mix_kernel,
        out_shape=jax.ShapeDtypeStruct((rows, width), BF16),
        in_specs=[IN_SMEM] + [IN_VMEM] * 8,
        out_specs=IN_VMEM,
        compiler_params=pltpu.CompilerParams(vmem_limit_bytes=40 * 2**20),
        cost_estimate=pl.CostEstimate(flops=16 * rows * chans * width, bytes_accessed=16 * rows * chans + 16 * chans * width, transcendentals=0),
        name="mix",
    )(place, own, theirs, near, far, mid_own, mid_other, w_mine, w_theirs)


def send(value, axis, pairs):
    return lax.ppermute(value, axis, pairs)


def shift_up(size, distance):
    return [(i, i + distance) for i in range(size - distance)]


class Routes:
    def __init__(self, chips, xs, zs):
        self.cores = [(i, i ^ 1) for i in range(2 * chips)]
        shards = xs * zs
        self.x, self.z = [], []
        for ch in range(2 * chips):
            way = 1 - 2 * (ch % 2)
            for x in range(xs):
                for z in range(zs):
                    here = ch * shards + x * zs + z
                    self.x.append((here, ch * shards + (x + way) % xs * zs + z))
                    self.z.append((here, ch * shards + x * zs + (z + way) % zs))
        self.y = [(2 * i + c, 2 * ((i + 1 - 2 * c) % chips) + c) for i in range(chips) for c in range(2)]
        self.across = [[(2 * i + c, 2 * ((i + k) % chips) + c) for i in range(chips) for c in range(2)] for k in range(chips)]

    def swap(self, v):
        return send(v, "ch", self.cores)

    def along_x(self, v):
        return send(v, ("ch", "seq"), self.x)

    def along_z(self, v):
        return send(v, ("ch", "seq"), self.z)

    def along_y(self, v):
        return send(v, "ch", self.y)


def joined(core, own, other, axis):
    return jnp.where(core == 0, jnp.concatenate([own, other], axis), jnp.concatenate([other, own], axis))


def half_of(core, value):
    half = value.shape[1] // 2
    return lax.dynamic_slice_in_dim(value, core * half, half, axis=1)


def gather_rows_first(routes, core, mine):
    depth = mine.shape[0]
    chip = jnp.stack([mine, routes.swap(mine)])
    z1, x1 = routes.along_z(chip), routes.along_x(chip)
    z2 = routes.along_z(z1)
    xh = routes.along_x(half_of(core, x1))
    o1 = routes.swap(z1)
    opposite = joined(core, xh, routes.swap(xh)[::-1], 1)
    n1 = routes.along_x(jnp.concatenate([z1, o1[::-1]], 1))
    z3 = routes.along_z(z2)
    f1 = routes.along_z(opposite)
    o2 = routes.swap(z2)
    n2 = routes.along_x(jnp.concatenate([z2, o2[::-1]], 1))
    z4 = routes.along_z(half_of(core, z3))
    f2 = routes.along_z(f1)
    o3 = routes.swap(jnp.concatenate([z3, z4], 1))
    across = joined(core, z4, o3[::-1, depth:], 1)
    n3 = routes.along_x(jnp.concatenate([z3, o3[::-1, :depth], across], 1))
    f3 = routes.along_z(f2)
    f4 = routes.along_z(half_of(core, f3))
    of = routes.swap(jnp.concatenate([f1[1], f2[1], f3[1], f4[1]], 0))
    on = routes.swap(jnp.concatenate([x1[1], n1[1], n2[1]], 0))
    on3 = routes.swap(n3[1])
    sources = [mine, z1, o1, z2, o2, z3, o3, z4, x1, n1, n2, n3, opposite, f1, f2, f3, f4, of, on, on3]
    moves = [(0, (), 0, depth, 0, 0, None)]
    for k, (own, other) in enumerate([(1, 2), (3, 4), (5, 6)], 1):
        moves += [(own, (0,), 0, depth, 0, -k, None), (other, (1,), 0, depth, 0, k, None)]
    moves += [(7, (0,), 0, depth // 2, 0, 4, "own"), (6, (1,), depth, depth // 2, 0, 4, "other")]
    moves += [(8, (0,), 0, depth, -1, 0, None), (18, (), 0, depth, 1, 0, None)]
    for k in (1, 2):
        for i, dz in enumerate((-k, k)):
            moves.append((8 + k, (0,), i * depth, depth, -1, dz, None))
            moves.append((18, (), (2 * k - 1 + i) * depth, depth, 1, -dz, None))
    for i, dz in enumerate((-3, 3, 4)):
        moves.append((11, (0,), i * depth, depth, -1, dz, None))
        moves.append((19, (), i * depth, depth, 1, -dz, None))
    moves.append((12, (0,), 0, depth, 2, 0, None))
    for k in (1, 2, 3):
        moves += [(12 + k, (0,), 0, depth, 2, -k, None), (17, (), (k - 1) * depth, depth, 2, k, None)]
    moves += [(16, (0,), 0, depth // 2, 2, 4, "own"), (17, (), 3 * depth, depth // 2, 2, 4, "other")]
    return sources, moves


def gather_x_first(routes, core, mine):
    depth = mine.shape[0]
    chip = jnp.stack([mine, routes.swap(mine)])
    x1 = routes.along_x(chip)
    xh = routes.along_x(half_of(core, x1))
    o = routes.swap(jnp.concatenate([x1, xh], 1))
    opposite = joined(core, xh, o[::-1, depth:], 1)
    four = jnp.concatenate([chip, x1, opposite, o[::-1, :depth]], 1)
    z1 = routes.along_z(four)
    z2 = routes.along_z(z1)
    z3 = routes.along_z(z2)
    z4 = routes.along_z(lax.dynamic_slice_in_dim(z3, core * depth, 2 * depth, axis=1))
    oz = routes.swap(jnp.concatenate([z1[1], z2[1], z3[1], z4[1]], 0))
    sources = [four, z1, z2, z3, z4, oz]
    moves = []
    for i, dx in enumerate((0, -1, 2, 1)):
        moves.append((0, (0,), i * depth, depth, dx, 0, None))
        for k in (1, 2, 3):
            moves.append((k, (0,), i * depth, depth, dx, -k, None))
            moves.append((5, (), (4 * (k - 1) + i) * depth, depth, -dx, k, None))
    for i, (here, there) in enumerate([((0, -1), (1, 0)), ((-1, 2), (2, 1))]):
        moves.append((4, (0,), i * depth, depth, here, 4, None))
        moves.append((5, (), (12 + i) * depth, depth, there, 4, None))
    return sources, moves


def own_columns(routes, out_weight, chips, y, core):
    width = out_weight.shape[1] // chips
    parts = []
    for k in range(chips):
        block = lax.dynamic_slice_in_dim(out_weight, (y + k) % chips * width, width, axis=1)
        parts.append(block if k == 0 else send(block, "ch", routes.across[k]))
    parts = jnp.stack(parts)
    half = width // 2
    mine = lax.dynamic_slice_in_dim(parts, core * half, half, axis=2)
    other = lax.dynamic_slice_in_dim(parts, (1 - core) * half, half, axis=2)
    return mine, routes.swap(other)


def entering_state(last, starts, decay_shard, shard_at, rows, shards, most):
    state = send(last, "seq", shift_up(shards, 1))
    window = 1
    while window * rows < most:
        lo = (shard_at - window) * rows
        thru = jnp.where(jnp.any((starts >= lo) & (starts < shard_at * rows)), 0.0, 1.0)
        state = state + (thru * decay_shard**window) * send(state, "seq", shift_up(shards, window))
        window *= 2
    return state


def per_device(xs, zs, tokens, in_weight, short_weight, decay_rate, residue, out_weight, contig_lengths):
    rows, width = tokens.shape
    chans = in_weight.shape[2]
    shards, chips = lax.axis_size("seq"), lax.axis_size("ch") // 2
    shard_at, place_ch = lax.axis_index("seq"), lax.axis_index("ch")
    y, core = place_ch // 2, place_ch % 2
    block = 2 * LANES
    most = 6144
    routes = Routes(chips, xs, zs)
    place = jnp.stack([shard_at // zs, shard_at % zs, core]).astype(jnp.int32)

    grouped = in_weight.reshape(-1, 3, chans // block, block)
    kv = jnp.concatenate([grouped[:, 1], grouped[:, 2]], axis=2).reshape(-1, 2 * chans)
    kv_sources, kv_moves = gather_rows_first(routes, core, kv)
    q_sources, q_moves = gather_x_first(routes, core, in_weight[:, 0])
    halo = send(tokens[rows - HALO :], "seq", shift_up(shards, 1))
    w_mine, w_theirs = own_columns(routes, out_weight, chips, y, core)

    starts, keep, mask2, keep_s, tail, thru = flags(contig_lengths, shard_at, rows)
    coef = residue * jnp.sqrt(-jnp.expm1(-2.0 * decay_rate))
    d = jnp.exp(-decay_rate)
    d_chunk = jnp.exp(-decay_rate * (rows // CHUNKS))
    d_shard = jnp.exp(-decay_rate * rows)
    kw, vw, qw = short_weight[1], short_weight[2], short_weight[0]
    drive, ends, last = call_drive(place, tokens, halo, kv_sources, kv_moves, kw, vw, keep, mask2, tail, thru, d, d_chunk, block)
    enter = entering_state(last, starts, d_shard, shard_at, rows, shards, most)
    fq = call_query(place, tokens, halo, q_sources, q_moves, qw, keep, mask2)
    gated = call_gate(drive, ends, enter, fq, keep_s, thru, d, d_chunk, coef, block)

    theirs = routes.swap(gated)
    near = routes.along_y(jnp.stack([gated, theirs]))
    mid = routes.along_y(half_of(core, near))
    far = routes.swap(near)
    mid_other = routes.swap(mid)
    return call_mix(place, gated, theirs, near, far, mid, mid_other, w_mine, w_theirs)


def solution(mesh):
    placed = (
        P("seq", None),
        P("seq", None, "ch"),
        P(None, None, "ch"),
        P(None, "ch"),
        P(None, "ch"),
        P("ch", None),
        P(),
    )
    return jax.shard_map(
        functools.partial(per_device, 4, 8), mesh=mesh, in_specs=placed, out_specs=P("seq", "ch"), check_vma=False
    )
```

```python
import functools
import jax
import jax.numpy as jnp
from jax import lax
from jax.experimental import pallas as pl
from jax.experimental.pallas import tpu as pltpu
from jax.sharding import PartitionSpec as P

F32, BF16 = jnp.float32, jnp.bfloat16
HALO = 16
CHUNKS = 8
LANES = 128
IN_VMEM = pl.BlockSpec(memory_space=pltpu.VMEM)
IN_SMEM = pl.BlockSpec(memory_space=pltpu.SMEM)


def land_kernel(moves, count, depth, place, *refs):
    sources, whole, sem = refs[:count], refs[-2], refs[-1]
    x, z, core = place[0], place[1], place[2]
    pick = lambda pair: pair[0] if pair[0] == pair[1] else jnp.where(core == 0, pair[0], pair[1])
    copies = []
    for source, by_core, row, rows, dx, dz, half in moves:
        at = (lax.rem(x + pick(dx) + 4, 4) * 8 + lax.rem(z + pick(dz) + 8, 8)) * depth
        if half is not None:
            at = at + (core if half == "own" else 1 - core) * rows
        ref = sources[source].at[core] if by_core else sources[source]
        to = whole.at[pl.ds(pl.multiple_of(at, 16), rows)]
        copies.append(pltpu.make_async_copy(ref.at[pl.ds(row, rows)], to, sem))
    for c in copies:
        c.start()
    for c in copies:
        c.wait()


def land(place, whole, sources, moves, depth, width):
    ins = [place, *sources] + ([] if whole is None else [whole])
    bytes_moved = 2 * 2 * width * sum(move[3] for move in moves)
    return pl.pallas_call(
        functools.partial(land_kernel, moves, len(sources), depth),
        out_shape=jax.ShapeDtypeStruct((32 * depth, width), BF16),
        in_specs=[IN_SMEM] + [pl.BlockSpec(memory_space=pl.ANY)] * (len(ins) - 1),
        out_specs=pl.BlockSpec(memory_space=pl.ANY),
        scratch_shapes=[pltpu.SemaphoreType.DMA],
        input_output_aliases={} if whole is None else {len(ins) - 1: 0},
        compiler_params=pltpu.CompilerParams(vmem_limit_bytes=2**20),
        cost_estimate=pl.CostEstimate(flops=0, bytes_accessed=bytes_moved, transcendentals=0),
        name="land",
    )(*ins)


def project(tok, weight, cols, acc, step=2048):
    def one(i):
        at = pl.ds(pl.multiple_of(i * step, step), step)
        return jnp.dot(tok[:, at], weight[at, cols], preferred_element_type=F32)

    acc[...] = one(0)

    @pl.loop(1, weight.shape[0] // step)
    def _(i):
        acc[...] += one(i)


def short_filter(acc, cols, taps, keep, mask2, r0, rows):
    window = acc[pl.ds(pl.multiple_of(HALO - 8 + r0, 8), rows + 8), cols]
    cur, one, two = window[8:], window[7:-1], window[6:-2]
    return taps[0:1] * cur + keep * (taps[1:2] * one) + mask2 * (taps[2:3] * two)


def drive_kernel(block, tok, whole, *refs):
    kw, vw, keep_ref, mask2_ref, tail_ref, thru_ref, d_ref, dchunk_ref = refs[:8]
    u_ref, end_ref, last_ref, acc, drive, ends = refs[8:]
    steps = u_ref.shape[1]
    modes = d_ref.shape[0]
    blocks = d_ref.shape[1] // block
    for b in range(blocks):
        project(tok, whole, pl.ds(b * 2 * block, 2 * block), acc)
        for s in range(block // LANES):
            g = b * (block // LANES) + s
            at = pl.ds(g * LANES, LANES)
            kc = pl.ds(s * LANES, LANES)
            vc = pl.ds(block + s * LANES, LANES)

            @pl.loop(0, CHUNKS)
            def _(j):
                r0 = pl.multiple_of(j * steps, 8)
                keep, mask2 = keep_ref[pl.ds(r0, steps), :], mask2_ref[pl.ds(r0, steps), :]
                fk = short_filter(acc, kc, kw[:, at], keep, mask2, r0, steps)
                fv = short_filter(acc, vc, vw[:, at], keep, mask2, r0, steps)
                drive[pl.ds(r0, steps), :] = fk * fv

            d = [jnp.broadcast_to(d_ref[pl.ds(m, 1), at], (CHUNKS, LANES)) for m in range(modes)]

            def step(t, state):
                u = drive[pl.ds(t, CHUNKS, stride=steps), :]
                u_ref[g, t] = u
                u = u * tail_ref[t]
                return tuple(d[m] * state[m] + u for m in range(modes))

            zero = jnp.zeros((CHUNKS, LANES), F32)
            state = lax.fori_loop(0, steps, step, (zero,) * modes, unroll=8)
            for m in range(modes):
                ends[m] = state[m]
            dc = dchunk_ref[:, at]
            enter = jnp.zeros((modes, LANES), F32)
            for j in range(CHUNKS):
                mine = ends[:, j, :]
                end_ref[:, j, at] = mine
                enter = dc * (enter * thru_ref[pl.ds(j, 1), :]) + mine
            last_ref[:, at] = enter


def query_kernel(tok, whole, qw, keep_ref, mask2_ref, fq_ref, acc):
    chans = fq_ref.shape[1]
    project(tok, whole, pl.ds(whole.shape[1] - chans, chans), acc)
    rows, chans = fq_ref.shape
    steps = rows // CHUNKS
    for s in range(chans // LANES):
        c = pl.ds(s * LANES, LANES)

        @pl.loop(0, CHUNKS)
        def _(j):
            r0 = pl.multiple_of(j * steps, 8)
            keep, mask2 = keep_ref[pl.ds(r0, steps), :], mask2_ref[pl.ds(r0, steps), :]
            fq_ref[pl.ds(r0, steps), c] = short_filter(acc, c, qw[:, c], keep, mask2, r0, steps)


def gate_kernel(u_ref, end_ref, enter_ref, fq_ref, keep_ref, thru_ref, d_ref, dchunk_ref, coef_ref, out_ref, states, long):
    rows, block = fq_ref.shape
    steps = rows // CHUNKS
    modes = d_ref.shape[0]
    for s in range(block // LANES):
        c = pl.ds(s * LANES, LANES)
        dc = dchunk_ref[:, c]
        enter = enter_ref[:, c]
        for j in range(CHUNKS):
            states[:, j, :] = enter
            enter = dc * (enter * thru_ref[pl.ds(j, 1), :]) + end_ref[:, j, c]
        d = [jnp.broadcast_to(d_ref[pl.ds(m, 1), c], (CHUNKS, LANES)) for m in range(modes)]
        coef = [jnp.broadcast_to(coef_ref[pl.ds(m, 1), c], (CHUNKS, LANES)) for m in range(modes)]

        def step(t, state):
            at = pl.ds(t, CHUNKS, stride=steps)
            u, keep = u_ref[s, t], keep_ref[t]
            state = tuple(d[m] * (keep * state[m]) + u for m in range(modes))
            terms = [coef[m] * state[m] for m in range(modes)]
            while len(terms) > 1:
                terms = [a + b for a, b in zip(terms[::2], terms[1::2])]
            long[at, :] = terms[0]
            return state

        lax.fori_loop(0, steps, step, tuple(states[m] for m in range(modes)), unroll=2)

        @pl.loop(0, CHUNKS)
        def _(j):
            at = pl.ds(pl.multiple_of(j * steps, 16), steps)
            out_ref[at, c] = (fq_ref[at, c] * long[at, :]).astype(BF16)


def call_drive(tokens, whole, kw, vw, keep, mask2, tail, thru, d, dchunk, block):
    rows, width = tokens.shape[0] - HALO, tokens.shape[1]
    modes, chans = d.shape
    return pl.pallas_call(
        functools.partial(drive_kernel, block),
        out_shape=[
            jax.ShapeDtypeStruct((chans // LANES, rows // CHUNKS, CHUNKS, LANES), F32),
            jax.ShapeDtypeStruct((modes, CHUNKS, chans), F32),
            jax.ShapeDtypeStruct((modes, chans), F32),
        ],
        in_specs=[IN_VMEM] * 10,
        out_specs=[IN_VMEM] * 3,
        scratch_shapes=[
            pltpu.VMEM((HALO + rows, 2 * block), F32),
            pltpu.VMEM((rows, LANES), F32),
            pltpu.VMEM((modes, CHUNKS, LANES), F32),
        ],
        compiler_params=pltpu.CompilerParams(vmem_limit_bytes=12 * 2**20),
        cost_estimate=pl.CostEstimate(flops=8 * rows * width * chans, bytes_accessed=2 * width * (rows + 2 * chans), transcendentals=0),
        name="drive",
    )(tokens, whole, kw, vw, keep, mask2, tail, thru, d, dchunk)


def call_query(tokens, whole, qw, keep, mask2):
    rows, width = tokens.shape[0] - HALO, tokens.shape[1]
    chans = qw.shape[1]
    return pl.pallas_call(
        query_kernel,
        out_shape=jax.ShapeDtypeStruct((rows, chans), F32),
        in_specs=[IN_VMEM] * 5,
        out_specs=IN_VMEM,
        scratch_shapes=[pltpu.VMEM((HALO + rows, chans), F32)],
        compiler_params=pltpu.CompilerParams(vmem_limit_bytes=12 * 2**20),
        cost_estimate=pl.CostEstimate(flops=4 * rows * width * chans, bytes_accessed=2 * width * (rows + chans), transcendentals=0),
        name="query",
    )(tokens, whole, qw, keep, mask2)


def call_gate(u, ends, enter, fq, keep, thru, d, dchunk, coef, block):
    rows, chans = fq.shape
    modes = d.shape[0]
    fixed = lambda a: pl.BlockSpec(a.shape, lambda b: (0,) * a.ndim)
    per_chan = lambda a: pl.BlockSpec((a.shape[0], block), lambda b: (0, b))
    return pl.pallas_call(
        gate_kernel,
        grid=(chans // block,),
        out_shape=jax.ShapeDtypeStruct((rows, chans), BF16),
        in_specs=[
            pl.BlockSpec((block // LANES, rows // CHUNKS, CHUNKS, LANES), lambda b: (b, 0, 0, 0)),
            pl.BlockSpec((modes, CHUNKS, block), lambda b: (0, 0, b)),
            per_chan(enter), per_chan(fq), fixed(keep), fixed(thru), per_chan(d), per_chan(dchunk), per_chan(coef),
        ],
        out_specs=pl.BlockSpec((rows, block), lambda b: (0, b)),
        scratch_shapes=[pltpu.VMEM((modes, CHUNKS, LANES), F32), pltpu.VMEM((rows, LANES), F32)],
        compiler_params=pltpu.CompilerParams(vmem_limit_bytes=8 * 2**20),
        cost_estimate=pl.CostEstimate(flops=5 * rows * modes * chans, bytes_accessed=10 * rows * chans, transcendentals=0),
        name="gate",
    )(u, ends, enter, fq, keep, thru, d, dchunk, coef)


def flags(contig_lengths, shard_at, rows):
    starts = jnp.cumsum(contig_lengths) - contig_lengths
    base = shard_at * rows
    position = base - 1 + jnp.arange(rows + 1, dtype=jnp.int32)
    first = jnp.any(position[:, None] == starts[None, :], axis=1)
    keep_ext = jnp.where(first, 0.0, 1.0).astype(F32)
    keep = keep_ext[1:]
    mask2 = keep * keep_ext[:-1]
    steps = rows // CHUNKS
    here = position[1:, None]
    chunk_end = base + (jnp.arange(rows, dtype=jnp.int32)[:, None] // steps + 1) * steps
    tail = jnp.where(jnp.any((starts[None] > here) & (starts[None] < chunk_end), axis=1), 0.0, 1.0).astype(F32)
    lo = base + jnp.arange(CHUNKS, dtype=jnp.int32)[:, None] * steps
    thru = jnp.where(jnp.any((starts[None] >= lo) & (starts[None] < lo + steps), axis=1), 0.0, 1.0).astype(F32)
    wide = lambda a: jnp.broadcast_to(a[:, None], (a.shape[0], LANES))
    slots = lambda a: wide(a).reshape(CHUNKS, steps, LANES).transpose(1, 0, 2)
    return starts, wide(keep), wide(mask2), slots(keep), slots(tail), wide(thru)


def send(value, axis, pairs):
    return lax.ppermute(value, axis, pairs)


def shift_up(size, distance):
    return [(i, i + distance) for i in range(size - distance)]


class Routes:
    def __init__(self, chips, xs, zs):
        self.cores = [(i, i ^ 1) for i in range(2 * chips)]
        shards = xs * zs
        self.x, self.z = [], []
        for ch in range(2 * chips):
            way = 1 - 2 * (ch % 2)
            for x in range(xs):
                for z in range(zs):
                    here = ch * shards + x * zs + z
                    self.x.append((here, ch * shards + (x + way) % xs * zs + z))
                    self.z.append((here, ch * shards + x * zs + (z + way) % zs))
        self.up = [(x * zs + z, (x + 1) % xs * zs + z) for x in range(xs) for z in range(zs)]
        self.down = [(b, a) for a, b in self.up]
        self.x_ahead = [(x * zs + z, (x + 1) * zs + z) for x in range(xs - 1) for z in range(zs)]
        self.y = [(2 * i + c, 2 * ((i + 1 - 2 * c) % chips) + c) for i in range(chips) for c in range(2)]

    def swap(self, v):
        return send(v, "ch", self.cores)

    def along_x(self, v):
        return send(v, ("ch", "seq"), self.x)

    def along_z(self, v):
        return send(v, ("ch", "seq"), self.z)

    def along_y(self, v):
        return send(v, "ch", self.y)

    def next_x(self, v):
        return send(v, "seq", self.x_ahead)

    def up_x(self, v):
        return send(v, "seq", self.up)

    def down_x(self, v):
        return send(v, "seq", self.down)


def joined(core, own, other, axis):
    return jnp.where(core == 0, jnp.concatenate([own, other], axis), jnp.concatenate([other, own], axis))


def half_of(core, value):
    half = value.shape[1] // 2
    return lax.dynamic_slice_in_dim(value, core * half, half, axis=1)


def rel(k):
    return (k, -k)


def same(k):
    return (k, k)


class Arrived:
    def __init__(self, routes, core, place, depth):
        self.routes, self.core, self.place, self.depth, self.whole = routes, core, place, depth, None

    def exchange(self, held, alone=()):
        sources, moves, parts, pieces, row = [], [], [], [], 0
        for array, own in [*alone, *held]:
            moves += [(len(sources), array.ndim == 3, *piece) for piece in own]
            sources.append(array)
        for array, own in held:
            parts.append(lax.dynamic_index_in_dim(array, 1 - self.core, 0, keepdims=False))
            for at, rows, dx, dz, half in own:
                pieces.append((row + at, rows, dx[::-1], dz[::-1], {None: None, "own": "other"}[half]))
            row += array.shape[1]
        moves += [(len(sources), False, *piece) for piece in pieces]
        sources.append(self.routes.swap(jnp.concatenate(parts, 0)))
        self.whole = land(self.place, self.whole, sources, moves, self.depth, sources[-1].shape[1])


def gather_rows_first(routes, core, place, mine, early):
    depth = mine.shape[0]
    got = Arrived(routes, core, place, depth)
    whole = lambda dx, dz: [(0, depth, dx, dz, None)]
    half = lambda dx: [(0, depth // 2, dx, same(4), "own")]
    chip = joined(core, mine[None], routes.swap(mine)[None], 0)
    z1, x1 = routes.along_z(chip), routes.along_x(chip)
    x1, z1 = lax.optimization_barrier((x1, z1))
    xh = routes.along_x(half_of(core, x1))
    z2 = routes.along_z(z1)
    opposite = joined(core, xh, routes.swap(xh), 1)
    tied, _ = lax.optimization_barrier((z1, xh))
    u1, d1 = routes.up_x(tied), routes.down_x(tied)
    f1 = routes.along_z(opposite)
    u2, d2 = routes.up_x(z2), routes.down_x(z2)
    tied, f1 = lax.optimization_barrier((z2, f1))
    z3 = routes.along_z(tied)
    f2 = routes.along_z(f1)
    z4 = routes.along_z(half_of(core, z3))
    got.exchange(
        [(x1, whole(rel(-1), same(0))), (z1, whole(same(0), rel(-1))), (z2, whole(same(0), rel(-2)))],
        [(mine, whole(same(0), same(0))), (opposite, whole(same(2), same(0)))],
    )
    tied, _, early, got.whole = lax.optimization_barrier((z3, (u1, d1), early, got.whole))
    u3, d3 = routes.up_x(tied), routes.down_x(tied)
    f3 = routes.along_z(f2)
    tied, _ = lax.optimization_barrier((z4, (u2, d2)))
    u4, d4 = routes.up_x(tied), routes.down_x(tied)
    got.exchange([
        (u1, whole(same(-1), rel(-1))), (d1, whole(same(1), rel(-1))),
        (u2, whole(same(-1), rel(-2))), (d2, whole(same(1), rel(-2))),
        (z3, whole(same(0), rel(-3))), (z4, half(same(0))), (f1, whole(same(2), rel(-1))),
    ])
    f4 = routes.along_z(half_of(core, f3))
    got.exchange([
        (u3, whole(same(-1), rel(-3))), (d3, whole(same(1), rel(-3))),
        (f2, whole(same(2), rel(-2))), (f3, whole(same(2), rel(-3))),
    ])
    got.exchange([(u4, half(same(-1))), (d4, half(same(1))), (f4, half(same(2)))])
    return got.whole, early


def state_weights(routes, core, starts, decay_rate, shard_at, rows, zs, most):
    count = most // rows
    half = count // 2
    z = shard_at % zs
    k = jnp.arange(half + 1, dtype=jnp.int32)
    steps = jnp.where(core == 0, k, count - k)
    wrapped = jnp.where(core == 0, z < k, z + k >= zs)
    mine = jnp.where(core == 0, ~wrapped, wrapped) & (k > 0)
    counted = jnp.where(core == 0, True, (k > 0) & (k < half))
    ahead = jnp.where(k == 0, count, steps)
    at = jnp.stack([jnp.full_like(k, shard_at), jnp.full_like(k, shard_at + zs)])
    lo, hi = (at - ahead + 1) * rows, at * rows
    broken = jnp.any((starts >= lo[..., None]) & (starts < hi[..., None]), axis=2)
    used = jnp.stack([mine, ~mine]) & counted & ~broken
    both = joined(core, decay_rate[None], routes.swap(decay_rate)[None], 0)
    away = ((ahead - 1) * rows).astype(F32)
    return used.astype(F32)[:, :, None, None, None] * jnp.exp(-both[None] * away[:, None, None, None])[None]


def entering_state(routes, core, last, fq, weights):
    going = joined(core, last[None], routes.swap(last)[None], 0)
    sums = weights[:, 0] * going
    for k in range(1, weights.shape[1]):
        going = routes.along_z(going)
        if k == 1:
            going, fq = lax.optimization_barrier((going, fq))
        sums = sums + weights[:, k] * going
    pick = lambda c: lax.dynamic_index_in_dim(sums, c, 1, keepdims=False)
    total = pick(core) + routes.swap(pick(1 - core))
    return total[0] + routes.next_x(total[1]), fq


def sum_over_channels(gated, out_weight, routes, chips, y, core):
    rows = gated.shape[0]
    width = out_weight.shape[1] // (2 * chips)
    way = 1 - 2 * core
    halves = [gated[: rows // 2], gated[rows // 2 :]]
    dot = lambda a, b: jnp.dot(a, b, preferred_element_type=F32)
    totals = [None, None]
    for k in range(chips - 1, -1, -1):
        mine = lax.dynamic_slice_in_dim(out_weight, (2 * ((y + k * way) % chips) + core) * width, width, axis=1)
        other = lax.dynamic_slice_in_dim(out_weight, (2 * ((y - k * way) % chips) + 1 - core) * width, width, axis=1)
        for i, part in enumerate(halves):
            block = dot(part, mine) + routes.swap(dot(part, other).astype(BF16)).astype(F32)
            if totals[i] is not None:
                block = block + routes.along_y(totals[i]).astype(F32)
            totals[i] = block.astype(BF16)
    return jnp.concatenate(totals, 0)


def per_device(xs, zs, tokens, in_weight, short_weight, decay_rate, residue, out_weight, contig_lengths):
    rows, width = tokens.shape
    chans = in_weight.shape[2]
    shards, chips = lax.axis_size("seq"), lax.axis_size("ch") // 2
    shard_at, place_ch = lax.axis_index("seq"), lax.axis_index("ch")
    y, core = place_ch // 2, place_ch % 2
    block = 2 * LANES
    most = 6144
    routes = Routes(chips, xs, zs)
    place = jnp.stack([shard_at // zs, shard_at % zs, core]).astype(jnp.int32)

    grouped = in_weight.reshape(-1, 3, chans // block, block)
    kv = jnp.concatenate([grouped[:, 1], grouped[:, 2]], axis=2).reshape(-1, 2 * chans)
    own = jnp.concatenate([kv, in_weight[:, 0]], axis=1)
    starts, *masks = flags(contig_lengths, shard_at, rows)
    coef = residue * jnp.sqrt(-jnp.expm1(-2.0 * decay_rate))
    d = jnp.exp(-decay_rate)
    d_chunk = jnp.exp(-decay_rate * (rows // CHUNKS))
    weights = state_weights(routes, core, starts, decay_rate, shard_at, rows, zs, most)
    halo = send(tokens[rows - HALO :], "seq", shift_up(shards, 1))
    early = (jnp.concatenate([halo, tokens], axis=0), *masks, coef, d, d_chunk, weights)
    whole, early = gather_rows_first(routes, core, place, own, early)
    padded, keep, mask2, keep_s, tail, thru, coef, d, d_chunk, weights = early
    kw, vw, qw = short_weight[1], short_weight[2], short_weight[0]
    drive, ends, last = call_drive(padded, whole, kw, vw, keep, mask2, tail, thru, d, d_chunk, block)
    fq = call_query(padded, whole, qw, keep, mask2)
    enter, fq = entering_state(routes, core, last, fq, weights)
    gated = call_gate(drive, ends, enter, fq, keep_s, thru, d, d_chunk, coef, block)

    return sum_over_channels(gated, out_weight, routes, chips, y, core)


def solution(mesh):
    placed = (
        P("seq", None),
        P("seq", None, "ch"),
        P(None, None, "ch"),
        P(None, "ch"),
        P(None, "ch"),
        P("ch", None),
        P(),
    )
    return jax.shard_map(
        functools.partial(per_device, 4, 8), mesh=mesh, in_specs=placed, out_specs=P("seq", "ch"), check_vma=False
    )
```

```python
import functools
import jax
import jax.numpy as jnp
from jax import lax
from jax.experimental import pallas as pl
from jax.experimental.pallas import tpu as pltpu
from jax.sharding import PartitionSpec as P

F32, BF16 = jnp.float32, jnp.bfloat16
HALO = 16
CHUNKS = 8
LANES = 128
IN_VMEM = pl.BlockSpec(memory_space=pltpu.VMEM)
IN_SMEM = pl.BlockSpec(memory_space=pltpu.SMEM)


def land_kernel(moves, count, depth, place, *refs):
    sources, whole, sem = refs[:count], refs[-2], refs[-1]
    x, z, core = place[0], place[1], place[2]
    pick = lambda pair: pair[0] if pair[0] == pair[1] else jnp.where(core == 0, pair[0], pair[1])
    copies = []
    for source, by_core, row, rows, dx, dz, half in moves:
        at = (lax.rem(x + pick(dx) + 4, 4) * 8 + lax.rem(z + pick(dz) + 8, 8)) * depth
        if half is not None:
            at = at + (core if half == "own" else 1 - core) * rows
        ref = sources[source].at[core] if by_core else sources[source]
        to = whole.at[pl.ds(pl.multiple_of(at, 16), rows)]
        copies.append(pltpu.make_async_copy(ref.at[pl.ds(row, rows)], to, sem))
    for c in copies:
        c.start()
    for c in copies:
        c.wait()


def land(place, whole, sources, moves, depth, width):
    ins = [place, *sources] + ([] if whole is None else [whole])
    bytes_moved = 2 * 2 * width * sum(move[3] for move in moves)
    return pl.pallas_call(
        functools.partial(land_kernel, moves, len(sources), depth),
        out_shape=jax.ShapeDtypeStruct((32 * depth, width), BF16),
        in_specs=[IN_SMEM] + [pl.BlockSpec(memory_space=pl.ANY)] * (len(ins) - 1),
        out_specs=pl.BlockSpec(memory_space=pl.ANY),
        scratch_shapes=[pltpu.SemaphoreType.DMA],
        input_output_aliases={} if whole is None else {len(ins) - 1: 0},
        compiler_params=pltpu.CompilerParams(vmem_limit_bytes=2**20),
        cost_estimate=pl.CostEstimate(flops=0, bytes_accessed=bytes_moved, transcendentals=0),
        name="land",
    )(*ins)


def project(tok, weight, cols, acc, step=2048):
    def one(i):
        at = pl.ds(pl.multiple_of(i * step, step), step)
        return jnp.dot(tok[:, at], weight[at, cols], preferred_element_type=F32)

    acc[...] = one(0)

    @pl.loop(1, weight.shape[0] // step)
    def _(i):
        acc[...] += one(i)


def short_filter(acc, cols, taps, keep, mask2, r0, rows):
    window = acc[pl.ds(pl.multiple_of(HALO - 8 + r0, 8), rows + 8), cols]
    cur, one, two = window[8:], window[7:-1], window[6:-2]
    return taps[0:1] * cur + keep * (taps[1:2] * one) + mask2 * (taps[2:3] * two)


def drive_kernel(block, tok, whole, *refs):
    kw, vw, keep_ref, mask2_ref, tail_ref, thru_ref, rates = refs[:7]
    u_ref, end_ref, last_ref, acc, drive, ends = refs[7:]
    steps = u_ref.shape[1]
    modes, chans = rates.shape[1:]
    blocks = chans // block
    for i in range(3):
        end_ref[:, CHUNKS + i, :] = rates[i]
    for b in range(blocks):
        project(tok, whole, pl.ds(b * 2 * block, 2 * block), acc)
        for s in range(block // LANES):
            g = b * (block // LANES) + s
            at = pl.ds(g * LANES, LANES)
            kc = pl.ds(s * LANES, LANES)
            vc = pl.ds(block + s * LANES, LANES)

            @pl.loop(0, CHUNKS)
            def _(j):
                r0 = pl.multiple_of(j * steps, 8)
                keep, mask2 = keep_ref[pl.ds(r0, steps), :], mask2_ref[pl.ds(r0, steps), :]
                fk = short_filter(acc, kc, kw[:, at], keep, mask2, r0, steps)
                fv = short_filter(acc, vc, vw[:, at], keep, mask2, r0, steps)
                drive[pl.ds(r0, steps), :] = fk * fv

            d = [jnp.broadcast_to(rates[0, pl.ds(m, 1), at], (CHUNKS, LANES)) for m in range(modes)]

            def step(t, state):
                u = drive[pl.ds(t, CHUNKS, stride=steps), :]
                u_ref[g, t] = u
                u = u * tail_ref[t]
                return tuple(d[m] * state[m] + u for m in range(modes))

            zero = jnp.zeros((CHUNKS, LANES), F32)
            state = lax.fori_loop(0, steps, step, (zero,) * modes, unroll=8)
            for m in range(modes):
                ends[m] = state[m]
            dc = rates[1, :, at]
            enter = jnp.zeros((modes, LANES), F32)
            for j in range(CHUNKS):
                mine = ends[:, j, :]
                end_ref[:, j, at] = mine
                enter = dc * (enter * thru_ref[pl.ds(j, 1), :]) + mine
            last_ref[:, at] = enter


def query_kernel(tok, whole, qw, keep_ref, mask2_ref, fq_ref, acc):
    chans = fq_ref.shape[1]
    project(tok, whole, pl.ds(whole.shape[1] - chans, chans), acc)
    rows, chans = fq_ref.shape
    steps = rows // CHUNKS
    for s in range(chans // LANES):
        c = pl.ds(s * LANES, LANES)

        @pl.loop(0, CHUNKS)
        def _(j):
            r0 = pl.multiple_of(j * steps, 8)
            keep, mask2 = keep_ref[pl.ds(r0, steps), :], mask2_ref[pl.ds(r0, steps), :]
            fq_ref[pl.ds(r0, steps), c] = short_filter(acc, c, qw[:, c], keep, mask2, r0, steps)


def gate_kernel(u_ref, end_ref, enter_ref, fq_ref, keep_ref, thru_ref, out_ref, states, long):
    rows, block = fq_ref.shape
    steps = rows // CHUNKS
    modes = end_ref.shape[0]
    for s in range(block // LANES):
        c = pl.ds(s * LANES, LANES)
        dc = end_ref[:, CHUNKS + 1, c]
        enter = enter_ref[:, c]
        for j in range(CHUNKS):
            states[:, j, :] = enter
            enter = dc * (enter * thru_ref[pl.ds(j, 1), :]) + end_ref[:, j, c]
        d = [jnp.broadcast_to(end_ref[m, pl.ds(CHUNKS, 1), c], (CHUNKS, LANES)) for m in range(modes)]
        coef = [jnp.broadcast_to(end_ref[m, pl.ds(CHUNKS + 2, 1), c], (CHUNKS, LANES)) for m in range(modes)]

        def step(t, state):
            at = pl.ds(t, CHUNKS, stride=steps)
            u, keep = u_ref[s, t], keep_ref[t]
            state = tuple(d[m] * (keep * state[m]) + u for m in range(modes))
            terms = [coef[m] * state[m] for m in range(modes)]
            while len(terms) > 1:
                terms = [a + b for a, b in zip(terms[::2], terms[1::2])]
            long[at, :] = terms[0]
            return state

        lax.fori_loop(0, steps, step, tuple(states[m] for m in range(modes)), unroll=2)

        @pl.loop(0, CHUNKS)
        def _(j):
            at = pl.ds(pl.multiple_of(j * steps, 16), steps)
            out_ref[at, c] = (fq_ref[at, c] * long[at, :]).astype(BF16)


def call_drive(tokens, whole, kw, vw, keep, mask2, tail, thru, rates, block):
    rows, width = tokens.shape[0] - HALO, tokens.shape[1]
    modes, chans = rates.shape[1:]
    return pl.pallas_call(
        functools.partial(drive_kernel, block),
        out_shape=[
            jax.ShapeDtypeStruct((chans // LANES, rows // CHUNKS, CHUNKS, LANES), F32),
            jax.ShapeDtypeStruct((modes, CHUNKS + 3, chans), F32),
            jax.ShapeDtypeStruct((modes, chans), F32),
        ],
        in_specs=[IN_VMEM] * 9,
        out_specs=[IN_VMEM] * 3,
        scratch_shapes=[
            pltpu.VMEM((HALO + rows, 2 * block), F32),
            pltpu.VMEM((rows, LANES), F32),
            pltpu.VMEM((modes, CHUNKS, LANES), F32),
        ],
        compiler_params=pltpu.CompilerParams(vmem_limit_bytes=12 * 2**20),
        cost_estimate=pl.CostEstimate(flops=8 * rows * width * chans, bytes_accessed=2 * width * (rows + 2 * chans), transcendentals=0),
        name="drive",
    )(tokens, whole, kw, vw, keep, mask2, tail, thru, rates)


def call_query(tokens, whole, qw, keep, mask2):
    rows, width = tokens.shape[0] - HALO, tokens.shape[1]
    chans = qw.shape[1]
    return pl.pallas_call(
        query_kernel,
        out_shape=jax.ShapeDtypeStruct((rows, chans), F32),
        in_specs=[IN_VMEM] * 5,
        out_specs=IN_VMEM,
        scratch_shapes=[pltpu.VMEM((HALO + rows, chans), F32)],
        compiler_params=pltpu.CompilerParams(vmem_limit_bytes=12 * 2**20),
        cost_estimate=pl.CostEstimate(flops=4 * rows * width * chans, bytes_accessed=2 * width * (rows + chans), transcendentals=0),
        name="query",
    )(tokens, whole, qw, keep, mask2)


def call_gate(u, ends, enter, fq, keep, thru, block):
    rows, chans = fq.shape
    modes, held = ends.shape[:2]
    fixed = lambda a: pl.BlockSpec(a.shape, lambda b: (0,) * a.ndim)
    per_chan = lambda a: pl.BlockSpec((a.shape[0], block), lambda b: (0, b))
    return pl.pallas_call(
        gate_kernel,
        grid=(chans // block,),
        out_shape=jax.ShapeDtypeStruct((rows, chans), BF16),
        in_specs=[
            pl.BlockSpec((block // LANES, rows // CHUNKS, CHUNKS, LANES), lambda b: (b, 0, 0, 0)),
            pl.BlockSpec((modes, held, block), lambda b: (0, 0, b)),
            per_chan(enter), per_chan(fq), fixed(keep), fixed(thru),
        ],
        out_specs=pl.BlockSpec((rows, block), lambda b: (0, b)),
        scratch_shapes=[pltpu.VMEM((modes, CHUNKS, LANES), F32), pltpu.VMEM((rows, LANES), F32)],
        compiler_params=pltpu.CompilerParams(vmem_limit_bytes=8 * 2**20),
        cost_estimate=pl.CostEstimate(flops=5 * rows * modes * chans, bytes_accessed=10 * rows * chans, transcendentals=0),
        name="gate",
    )(u, ends, enter, fq, keep, thru)


def flags(contig_lengths, shard_at, rows):
    starts = jnp.cumsum(contig_lengths) - contig_lengths
    base = shard_at * rows
    position = base - 1 + jnp.arange(rows + 1, dtype=jnp.int32)
    first = jnp.any(position[:, None] == starts[None, :], axis=1)
    keep_ext = jnp.where(first, 0.0, 1.0).astype(F32)
    keep = keep_ext[1:]
    mask2 = keep * keep_ext[:-1]
    steps = rows // CHUNKS
    here = position[1:, None]
    chunk_end = base + (jnp.arange(rows, dtype=jnp.int32)[:, None] // steps + 1) * steps
    tail = jnp.where(jnp.any((starts[None] > here) & (starts[None] < chunk_end), axis=1), 0.0, 1.0).astype(F32)
    lo = base + jnp.arange(CHUNKS, dtype=jnp.int32)[:, None] * steps
    thru = jnp.where(jnp.any((starts[None] >= lo) & (starts[None] < lo + steps), axis=1), 0.0, 1.0).astype(F32)
    wide = lambda a: jnp.broadcast_to(a[:, None], (a.shape[0], LANES))
    slots = lambda a: wide(a).reshape(CHUNKS, steps, LANES).transpose(1, 0, 2)
    return starts, wide(keep), wide(mask2), slots(keep), slots(tail), wide(thru)


def send(value, axis, pairs):
    return lax.ppermute(value, axis, pairs)


def shift_up(size, distance):
    return [(i, i + distance) for i in range(size - distance)]


class Routes:
    def __init__(self, chips, xs, zs):
        self.cores = [(i, i ^ 1) for i in range(2 * chips)]
        shards = xs * zs
        self.x, self.z = [], []
        for ch in range(2 * chips):
            way = 1 - 2 * (ch % 2)
            for x in range(xs):
                for z in range(zs):
                    here = ch * shards + x * zs + z
                    self.x.append((here, ch * shards + (x + way) % xs * zs + z))
                    self.z.append((here, ch * shards + x * zs + (z + way) % zs))
        self.up = [(x * zs + z, (x + 1) % xs * zs + z) for x in range(xs) for z in range(zs)]
        self.down = [(b, a) for a, b in self.up]
        self.x_ahead = [(x * zs + z, (x + 1) * zs + z) for x in range(xs - 1) for z in range(zs)]
        self.y = [(2 * i + c, 2 * ((i + 1 - 2 * c) % chips) + c) for i in range(chips) for c in range(2)]

    def swap(self, v):
        return send(v, "ch", self.cores)

    def along_x(self, v):
        return send(v, ("ch", "seq"), self.x)

    def along_z(self, v):
        return send(v, ("ch", "seq"), self.z)

    def along_y(self, v):
        return send(v, "ch", self.y)

    def next_x(self, v):
        return send(v, "seq", self.x_ahead)

    def up_x(self, v):
        return send(v, "seq", self.up)

    def down_x(self, v):
        return send(v, "seq", self.down)


def joined(core, own, other, axis):
    return jnp.where(core == 0, jnp.concatenate([own, other], axis), jnp.concatenate([other, own], axis))


def half_of(core, value):
    half = value.shape[1] // 2
    return lax.dynamic_slice_in_dim(value, core * half, half, axis=1)


def rel(k):
    return (k, -k)


def same(k):
    return (k, k)


class Arrived:
    def __init__(self, routes, core, place, depth):
        self.routes, self.core, self.place, self.depth, self.whole = routes, core, place, depth, None

    def exchange(self, held, alone=()):
        sources, moves, parts, pieces, row = [], [], [], [], 0
        for array, own in [*alone, *held]:
            moves += [(len(sources), array.ndim == 3, *piece) for piece in own]
            sources.append(array)
        for array, own in held:
            parts.append(lax.dynamic_index_in_dim(array, 1 - self.core, 0, keepdims=False))
            for at, rows, dx, dz, half in own:
                pieces.append((row + at, rows, dx[::-1], dz[::-1], {None: None, "own": "other"}[half]))
            row += array.shape[1]
        moves += [(len(sources), False, *piece) for piece in pieces]
        sources.append(self.routes.swap(jnp.concatenate(parts, 0)))
        self.whole = land(self.place, self.whole, sources, moves, self.depth, sources[-1].shape[1])


def gather_rows_first(routes, core, place, mine, early):
    depth = mine.shape[0]
    got = Arrived(routes, core, place, depth)
    whole = lambda dx, dz: [(0, depth, dx, dz, None)]
    half = lambda dx: [(0, depth // 2, dx, same(4), "own")]
    chip = joined(core, mine[None], routes.swap(mine)[None], 0)
    z1, x1 = routes.along_z(chip), routes.along_x(chip)
    x1, z1 = lax.optimization_barrier((x1, z1))
    xh = routes.along_x(half_of(core, x1))
    z2 = routes.along_z(z1)
    opposite = joined(core, xh, routes.swap(xh), 1)
    tied, _ = lax.optimization_barrier((z1, xh))
    u1, d1 = routes.up_x(tied), routes.down_x(tied)
    f1 = routes.along_z(opposite)
    u2, d2 = routes.up_x(z2), routes.down_x(z2)
    tied, f1 = lax.optimization_barrier((z2, f1))
    z3 = routes.along_z(tied)
    f2 = routes.along_z(f1)
    z4 = routes.along_z(half_of(core, z3))
    got.exchange(
        [(x1, whole(rel(-1), same(0))), (z1, whole(same(0), rel(-1))), (z2, whole(same(0), rel(-2)))],
        [(mine, whole(same(0), same(0))), (opposite, whole(same(2), same(0)))],
    )
    tied, _, early, got.whole = lax.optimization_barrier((z3, (u1, d1), early, got.whole))
    u3, d3 = routes.up_x(tied), routes.down_x(tied)
    f3 = routes.along_z(f2)
    tied, _ = lax.optimization_barrier((z4, (u2, d2)))
    u4, d4 = routes.up_x(tied), routes.down_x(tied)
    got.exchange([
        (u1, whole(same(-1), rel(-1))), (d1, whole(same(1), rel(-1))),
        (u2, whole(same(-1), rel(-2))), (d2, whole(same(1), rel(-2))),
        (z3, whole(same(0), rel(-3))), (z4, half(same(0))), (f1, whole(same(2), rel(-1))),
    ])
    f4 = routes.along_z(half_of(core, f3))
    got.exchange([
        (u3, whole(same(-1), rel(-3))), (d3, whole(same(1), rel(-3))),
        (f2, whole(same(2), rel(-2))), (f3, whole(same(2), rel(-3))),
    ])
    got.exchange([(u4, half(same(-1))), (d4, half(same(1))), (f4, half(same(2)))])
    return got.whole, early


def state_weights(routes, core, starts, decay_rate, shard_at, rows, zs, most):
    count = most // rows
    half = count // 2
    z = shard_at % zs
    k = jnp.arange(half + 1, dtype=jnp.int32)
    steps = jnp.where(core == 0, k, count - k)
    wrapped = jnp.where(core == 0, z < k, z + k >= zs)
    mine = jnp.where(core == 0, ~wrapped, wrapped) & (k > 0)
    counted = jnp.where(core == 0, True, (k > 0) & (k < half))
    ahead = jnp.where(k == 0, count, steps)
    at = jnp.stack([jnp.full_like(k, shard_at), jnp.full_like(k, shard_at + zs)])
    lo, hi = (at - ahead + 1) * rows, at * rows
    broken = jnp.any((starts >= lo[..., None]) & (starts < hi[..., None]), axis=2)
    used = jnp.stack([mine, ~mine]) & counted & ~broken
    both = joined(core, decay_rate[None], routes.swap(decay_rate)[None], 0)
    away = ((ahead - 1) * rows).astype(F32)
    return used.astype(F32)[:, :, None, None, None] * jnp.exp(-both[None] * away[:, None, None, None])[None]


def entering_state(routes, core, last, fq, weights):
    going = joined(core, last[None], routes.swap(last)[None], 0)
    sums = weights[:, 0] * going
    for k in range(1, weights.shape[1]):
        going = routes.along_z(going)
        if k == 1:
            going, fq = lax.optimization_barrier((going, fq))
        sums = sums + weights[:, k] * going
    pick = lambda c: lax.dynamic_index_in_dim(sums, c, 1, keepdims=False)
    total = pick(core) + routes.swap(pick(1 - core))
    return total[0] + routes.next_x(total[1]), fq


def sum_over_channels(gated, out_weight, routes, chips, y, core):
    rows = gated.shape[0]
    width = out_weight.shape[1] // (2 * chips)
    way = 1 - 2 * core
    halves = [gated[: rows // 2], gated[rows // 2 :]]
    dot = lambda a, b: jnp.dot(a, b, preferred_element_type=F32)
    totals = [None, None]
    for k in range(chips - 1, -1, -1):
        mine = lax.dynamic_slice_in_dim(out_weight, (2 * ((y + k * way) % chips) + core) * width, width, axis=1)
        other = lax.dynamic_slice_in_dim(out_weight, (2 * ((y - k * way) % chips) + 1 - core) * width, width, axis=1)
        for i, part in enumerate(halves):
            if totals[i] is not None:
                part, _ = lax.optimization_barrier((part, totals[i]))
            block = lax.optimization_barrier(dot(part, mine)) + routes.swap(dot(part, other).astype(BF16)).astype(F32)
            if totals[i] is not None:
                block = block + routes.along_y(totals[i]).astype(F32)
            totals[i] = block.astype(BF16)
    return jnp.concatenate(totals, 0)


def per_device(xs, zs, tokens, in_weight, short_weight, decay_rate, residue, out_weight, contig_lengths):
    rows, width = tokens.shape
    chans = in_weight.shape[2]
    shards, chips = lax.axis_size("seq"), lax.axis_size("ch") // 2
    shard_at, place_ch = lax.axis_index("seq"), lax.axis_index("ch")
    y, core = place_ch // 2, place_ch % 2
    block = 2 * LANES
    most = 6144
    routes = Routes(chips, xs, zs)
    place = jnp.stack([shard_at // zs, shard_at % zs, core]).astype(jnp.int32)

    grouped = in_weight.reshape(-1, 3, chans // block, block)
    kv = jnp.concatenate([grouped[:, 1], grouped[:, 2]], axis=2).reshape(-1, 2 * chans)
    own = jnp.concatenate([kv, in_weight[:, 0]], axis=1)
    starts, *masks = flags(contig_lengths, shard_at, rows)
    coef = residue * jnp.sqrt(-jnp.expm1(-2.0 * decay_rate))
    d = jnp.exp(-decay_rate)
    d_chunk = jnp.exp(-decay_rate * (rows // CHUNKS))
    weights = state_weights(routes, core, starts, decay_rate, shard_at, rows, zs, most)
    halo = send(tokens[rows - HALO :], "seq", shift_up(shards, 1))
    early = (jnp.concatenate([halo, tokens], axis=0), *masks, jnp.stack([d, d_chunk, coef]), weights)
    whole, early = gather_rows_first(routes, core, place, own, early)
    padded, keep, mask2, keep_s, tail, thru, rates, weights = early
    kw, vw, qw = short_weight[1], short_weight[2], short_weight[0]
    drive, ends, last = call_drive(padded, whole, kw, vw, keep, mask2, tail, thru, rates, block)
    fq = call_query(padded, whole, qw, keep, mask2)
    enter, fq = entering_state(routes, core, last, fq, weights)
    gated = call_gate(drive, ends, enter, fq, keep_s, thru, block)

    return sum_over_channels(gated, out_weight, routes, chips, y, core)


def solution(mesh):
    placed = (
        P("seq", None),
        P("seq", None, "ch"),
        P(None, None, "ch"),
        P(None, "ch"),
        P(None, "ch"),
        P("ch", None),
        P(),
    )
    return jax.shard_map(
        functools.partial(per_device, 4, 8), mesh=mesh, in_specs=placed, out_specs=P("seq", "ch"), check_vma=False
    )
```

```python
import functools
import jax
import jax.numpy as jnp
from jax import lax
from jax.experimental import pallas as pl
from jax.experimental.pallas import tpu as pltpu
from jax.sharding import PartitionSpec as P

F32, BF16 = jnp.float32, jnp.bfloat16
HALO = 16
CHUNKS = 8
LANES = 128
IN_VMEM = pl.BlockSpec(memory_space=pltpu.VMEM)
IN_SMEM = pl.BlockSpec(memory_space=pltpu.SMEM)


def land_kernel(moves, count, depth, place, *refs):
    sources, whole, sem = refs[:count], refs[-2], refs[-1]
    x, z, core = place[0], place[1], place[2]
    pick = lambda pair: pair[0] if pair[0] == pair[1] else jnp.where(core == 0, pair[0], pair[1])
    copies = []
    for source, by_core, row, rows, dx, dz, half in moves:
        at = (lax.rem(x + pick(dx) + 4, 4) * 8 + lax.rem(z + pick(dz) + 8, 8)) * depth
        if half is not None:
            at = at + (core if half == "own" else 1 - core) * rows
        ref = sources[source].at[core] if by_core else sources[source]
        to = whole.at[pl.ds(pl.multiple_of(at, 16), rows)]
        copies.append(pltpu.make_async_copy(ref.at[pl.ds(row, rows)], to, sem))
    for c in copies:
        c.start()
    for c in copies:
        c.wait()


def land(place, whole, sources, moves, depth, width):
    ins = [place, *sources] + ([] if whole is None else [whole])
    bytes_moved = 2 * 2 * width * sum(move[3] for move in moves)
    return pl.pallas_call(
        functools.partial(land_kernel, moves, len(sources), depth),
        out_shape=jax.ShapeDtypeStruct((32 * depth, width), BF16),
        in_specs=[IN_SMEM] + [pl.BlockSpec(memory_space=pl.ANY)] * (len(ins) - 1),
        out_specs=pl.BlockSpec(memory_space=pl.ANY),
        scratch_shapes=[pltpu.SemaphoreType.DMA],
        input_output_aliases={} if whole is None else {len(ins) - 1: 0},
        compiler_params=pltpu.CompilerParams(vmem_limit_bytes=2**20),
        cost_estimate=pl.CostEstimate(flops=0, bytes_accessed=bytes_moved, transcendentals=0),
        name="land",
    )(*ins)


def project(tok, weight, cols, acc, step=2048):
    def one(i):
        at = pl.ds(pl.multiple_of(i * step, step), step)
        return jnp.dot(tok[:, at], weight[at, cols], preferred_element_type=F32)

    acc[...] = one(0)

    @pl.loop(1, weight.shape[0] // step)
    def _(i):
        acc[...] += one(i)


def short_filter(acc, cols, taps, keep, mask2, r0, rows):
    window = acc[pl.ds(pl.multiple_of(HALO - 8 + r0, 8), rows + 8), cols]
    cur, one, two = window[8:], window[7:-1], window[6:-2]
    return taps[0:1] * cur + keep * (taps[1:2] * one) + mask2 * (taps[2:3] * two)


def drive_kernel(block, tok, whole, *refs):
    kw, vw, keep_ref, mask2_ref, tail_ref, thru_ref, rates = refs[:7]
    u_ref, end_ref, last_ref, acc, drive, ends = refs[7:]
    steps = u_ref.shape[1]
    modes, chans = rates.shape[1:]
    blocks = chans // block
    for i in range(3):
        end_ref[:, CHUNKS + i, :] = rates[i]
    for b in range(blocks):
        project(tok, whole, pl.ds(b * 2 * block, 2 * block), acc)
        for s in range(block // LANES):
            g = b * (block // LANES) + s
            at = pl.ds(g * LANES, LANES)
            kc = pl.ds(s * LANES, LANES)
            vc = pl.ds(block + s * LANES, LANES)

            @pl.loop(0, CHUNKS)
            def _(j):
                r0 = pl.multiple_of(j * steps, 8)
                keep, mask2 = keep_ref[pl.ds(r0, steps), :], mask2_ref[pl.ds(r0, steps), :]
                fk = short_filter(acc, kc, kw[:, at], keep, mask2, r0, steps)
                fv = short_filter(acc, vc, vw[:, at], keep, mask2, r0, steps)
                drive[pl.ds(r0, steps), :] = fk * fv

            d = [jnp.broadcast_to(rates[0, pl.ds(m, 1), at], (CHUNKS, LANES)) for m in range(modes)]

            def step(t, state):
                u = drive[pl.ds(t, CHUNKS, stride=steps), :]
                u_ref[g, t] = u
                u = u * tail_ref[t]
                return tuple(d[m] * state[m] + u for m in range(modes))

            zero = jnp.zeros((CHUNKS, LANES), F32)
            state = lax.fori_loop(0, steps, step, (zero,) * modes, unroll=8)
            for m in range(modes):
                ends[m] = state[m]
            dc = rates[1, :, at]
            enter = jnp.zeros((modes, LANES), F32)
            for j in range(CHUNKS):
                mine = ends[:, j, :]
                end_ref[:, j, at] = mine
                enter = dc * (enter * thru_ref[pl.ds(j, 1), :]) + mine
            last_ref[:, at] = enter


def query_kernel(tok, whole, qw, keep_ref, mask2_ref, fq_ref, acc):
    chans = fq_ref.shape[1]
    project(tok, whole, pl.ds(whole.shape[1] - chans, chans), acc)
    rows, chans = fq_ref.shape
    steps = rows // CHUNKS
    for s in range(chans // LANES):
        c = pl.ds(s * LANES, LANES)

        @pl.loop(0, CHUNKS)
        def _(j):
            r0 = pl.multiple_of(j * steps, 8)
            keep, mask2 = keep_ref[pl.ds(r0, steps), :], mask2_ref[pl.ds(r0, steps), :]
            fq_ref[pl.ds(r0, steps), c] = short_filter(acc, c, qw[:, c], keep, mask2, r0, steps)


def gate_kernel(u_ref, end_ref, enter_ref, fq_ref, keep_ref, thru_ref, out_ref, states, long):
    rows, block = fq_ref.shape
    steps = rows // CHUNKS
    modes = end_ref.shape[0]
    for s in range(block // LANES):
        c = pl.ds(s * LANES, LANES)
        dc = end_ref[:, CHUNKS + 1, c]
        enter = enter_ref[:, c]
        for j in range(CHUNKS):
            states[:, j, :] = enter
            enter = dc * (enter * thru_ref[pl.ds(j, 1), :]) + end_ref[:, j, c]
        d = [jnp.broadcast_to(end_ref[m, pl.ds(CHUNKS, 1), c], (CHUNKS, LANES)) for m in range(modes)]
        coef = [jnp.broadcast_to(end_ref[m, pl.ds(CHUNKS + 2, 1), c], (CHUNKS, LANES)) for m in range(modes)]

        def step(t, state):
            at = pl.ds(t, CHUNKS, stride=steps)
            u, keep = u_ref[s, t], keep_ref[t]
            state = tuple(d[m] * (keep * state[m]) + u for m in range(modes))
            terms = [coef[m] * state[m] for m in range(modes)]
            while len(terms) > 1:
                terms = [a + b for a, b in zip(terms[::2], terms[1::2])]
            long[at, :] = terms[0]
            return state

        lax.fori_loop(0, steps, step, tuple(states[m] for m in range(modes)), unroll=2)

        @pl.loop(0, CHUNKS)
        def _(j):
            at = pl.ds(pl.multiple_of(j * steps, 16), steps)
            out_ref[at, c] = (fq_ref[at, c] * long[at, :]).astype(BF16)


def call_drive(tokens, whole, kw, vw, keep, mask2, tail, thru, rates, block):
    rows, width = tokens.shape[0] - HALO, tokens.shape[1]
    modes, chans = rates.shape[1:]
    return pl.pallas_call(
        functools.partial(drive_kernel, block),
        out_shape=[
            jax.ShapeDtypeStruct((chans // LANES, rows // CHUNKS, CHUNKS, LANES), F32),
            jax.ShapeDtypeStruct((modes, CHUNKS + 3, chans), F32),
            jax.ShapeDtypeStruct((modes, chans), F32),
        ],
        in_specs=[IN_VMEM] * 9,
        out_specs=[IN_VMEM] * 3,
        scratch_shapes=[
            pltpu.VMEM((HALO + rows, 2 * block), F32),
            pltpu.VMEM((rows, LANES), F32),
            pltpu.VMEM((modes, CHUNKS, LANES), F32),
        ],
        compiler_params=pltpu.CompilerParams(vmem_limit_bytes=12 * 2**20),
        cost_estimate=pl.CostEstimate(flops=8 * rows * width * chans, bytes_accessed=2 * width * (rows + 2 * chans), transcendentals=0),
        name="drive",
    )(tokens, whole, kw, vw, keep, mask2, tail, thru, rates)


def call_query(tokens, whole, qw, keep, mask2):
    rows, width = tokens.shape[0] - HALO, tokens.shape[1]
    chans = qw.shape[1]
    return pl.pallas_call(
        query_kernel,
        out_shape=jax.ShapeDtypeStruct((rows, chans), F32),
        in_specs=[IN_VMEM] * 5,
        out_specs=IN_VMEM,
        scratch_shapes=[pltpu.VMEM((HALO + rows, chans), F32)],
        compiler_params=pltpu.CompilerParams(vmem_limit_bytes=12 * 2**20),
        cost_estimate=pl.CostEstimate(flops=4 * rows * width * chans, bytes_accessed=2 * width * (rows + chans), transcendentals=0),
        name="query",
    )(tokens, whole, qw, keep, mask2)


def call_gate(u, ends, enter, fq, keep, thru, block):
    rows, chans = fq.shape
    modes, held = ends.shape[:2]
    fixed = lambda a: pl.BlockSpec(a.shape, lambda b: (0,) * a.ndim)
    per_chan = lambda a: pl.BlockSpec((a.shape[0], block), lambda b: (0, b))
    return pl.pallas_call(
        gate_kernel,
        grid=(chans // block,),
        out_shape=jax.ShapeDtypeStruct((rows, chans), BF16),
        in_specs=[
            pl.BlockSpec((block // LANES, rows // CHUNKS, CHUNKS, LANES), lambda b: (b, 0, 0, 0)),
            pl.BlockSpec((modes, held, block), lambda b: (0, 0, b)),
            per_chan(enter), per_chan(fq), fixed(keep), fixed(thru),
        ],
        out_specs=pl.BlockSpec((rows, block), lambda b: (0, b)),
        scratch_shapes=[pltpu.VMEM((modes, CHUNKS, LANES), F32), pltpu.VMEM((rows, LANES), F32)],
        compiler_params=pltpu.CompilerParams(vmem_limit_bytes=8 * 2**20),
        cost_estimate=pl.CostEstimate(flops=5 * rows * modes * chans, bytes_accessed=10 * rows * chans, transcendentals=0),
        name="gate",
    )(u, ends, enter, fq, keep, thru)


def flags(contig_lengths, shard_at, rows):
    starts = jnp.cumsum(contig_lengths) - contig_lengths
    base = shard_at * rows
    position = base - 1 + jnp.arange(rows + 1, dtype=jnp.int32)
    first = jnp.any(position[:, None] == starts[None, :], axis=1)
    keep_ext = jnp.where(first, 0.0, 1.0).astype(F32)
    keep = keep_ext[1:]
    mask2 = keep * keep_ext[:-1]
    steps = rows // CHUNKS
    here = position[1:, None]
    chunk_end = base + (jnp.arange(rows, dtype=jnp.int32)[:, None] // steps + 1) * steps
    tail = jnp.where(jnp.any((starts[None] > here) & (starts[None] < chunk_end), axis=1), 0.0, 1.0).astype(F32)
    lo = base + jnp.arange(CHUNKS, dtype=jnp.int32)[:, None] * steps
    thru = jnp.where(jnp.any((starts[None] >= lo) & (starts[None] < lo + steps), axis=1), 0.0, 1.0).astype(F32)
    wide = lambda a: jnp.broadcast_to(a[:, None], (a.shape[0], LANES))
    slots = lambda a: wide(a).reshape(CHUNKS, steps, LANES).transpose(1, 0, 2)
    return starts, wide(keep), wide(mask2), slots(keep), slots(tail), wide(thru)


def send(value, axis, pairs):
    return lax.ppermute(value, axis, pairs)


def shift_up(size, distance):
    return [(i, i + distance) for i in range(size - distance)]


class Routes:
    def __init__(self, chips, xs, zs):
        self.cores = [(i, i ^ 1) for i in range(2 * chips)]
        shards = xs * zs
        self.x, self.z = [], []
        for ch in range(2 * chips):
            way = 1 - 2 * (ch % 2)
            for x in range(xs):
                for z in range(zs):
                    here = ch * shards + x * zs + z
                    self.x.append((here, ch * shards + (x + way) % xs * zs + z))
                    self.z.append((here, ch * shards + x * zs + (z + way) % zs))
        self.up = [(x * zs + z, (x + 1) % xs * zs + z) for x in range(xs) for z in range(zs)]
        self.down = [(b, a) for a, b in self.up]
        self.x_ahead = [(x * zs + z, (x + 1) * zs + z) for x in range(xs - 1) for z in range(zs)]
        self.y = [(2 * i + c, 2 * ((i + 1 - 2 * c) % chips) + c) for i in range(chips) for c in range(2)]

    def swap(self, v):
        return send(v, "ch", self.cores)

    def along_x(self, v):
        return send(v, ("ch", "seq"), self.x)

    def along_z(self, v):
        return send(v, ("ch", "seq"), self.z)

    def along_y(self, v):
        return send(v, "ch", self.y)

    def next_x(self, v):
        return send(v, "seq", self.x_ahead)

    def up_x(self, v):
        return send(v, "seq", self.up)

    def down_x(self, v):
        return send(v, "seq", self.down)


def joined(core, own, other, axis):
    return jnp.where(core == 0, jnp.concatenate([own, other], axis), jnp.concatenate([other, own], axis))


def half_of(core, value):
    half = value.shape[1] // 2
    return lax.dynamic_slice_in_dim(value, core * half, half, axis=1)


def rel(k):
    return (k, -k)


def same(k):
    return (k, k)


class Arrived:
    def __init__(self, routes, core, place, depth):
        self.routes, self.core, self.place, self.depth, self.whole = routes, core, place, depth, None

    def exchange(self, held, alone=()):
        sources, moves, parts, pieces, row = [], [], [], [], 0
        for array, own in [*alone, *held]:
            moves += [(len(sources), array.ndim == 3, *piece) for piece in own]
            sources.append(array)
        for array, own in held:
            parts.append(lax.dynamic_index_in_dim(array, 1 - self.core, 0, keepdims=False))
            for at, rows, dx, dz, half in own:
                pieces.append((row + at, rows, dx[::-1], dz[::-1], {None: None, "own": "other"}[half]))
            row += array.shape[1]
        moves += [(len(sources), False, *piece) for piece in pieces]
        sources.append(self.routes.swap(jnp.concatenate(parts, 0)))
        self.whole = land(self.place, self.whole, sources, moves, self.depth, sources[-1].shape[1])


def gather_rows_first(routes, core, place, mine, early):
    depth = mine.shape[0]
    got = Arrived(routes, core, place, depth)
    whole = lambda dx, dz: [(0, depth, dx, dz, None)]
    half = lambda dx: [(0, depth // 2, dx, same(4), "own")]
    chip = joined(core, mine[None], routes.swap(mine)[None], 0)
    chip, tail_rows = lax.optimization_barrier((chip, early[0]))
    z1, x1 = routes.along_z(chip), routes.along_x(chip)
    halo = send(tail_rows, "seq", shift_up(lax.axis_size("seq"), 1))
    x1, z1, halo = lax.optimization_barrier((x1, z1, halo))
    early = (jnp.concatenate([halo, early[1]], axis=0), *early[2:])
    xh = routes.along_x(half_of(core, x1))
    z2 = routes.along_z(z1)
    opposite = joined(core, xh, routes.swap(xh), 1)
    tied, _ = lax.optimization_barrier((z1, xh))
    u1, d1 = routes.up_x(tied), routes.down_x(tied)
    f1 = routes.along_z(opposite)
    u2, d2 = routes.up_x(z2), routes.down_x(z2)
    tied, f1 = lax.optimization_barrier((z2, f1))
    z3 = routes.along_z(tied)
    f2 = routes.along_z(f1)
    z4 = routes.along_z(half_of(core, z3))
    got.exchange(
        [(x1, whole(rel(-1), same(0))), (z1, whole(same(0), rel(-1))), (z2, whole(same(0), rel(-2)))],
        [(mine, whole(same(0), same(0))), (opposite, whole(same(2), same(0)))],
    )
    tied, _, early, got.whole = lax.optimization_barrier((z3, (u1, d1), early, got.whole))
    u3, d3 = routes.up_x(tied), routes.down_x(tied)
    f3 = routes.along_z(f2)
    tied, _ = lax.optimization_barrier((z4, (u2, d2)))
    u4, d4 = routes.up_x(tied), routes.down_x(tied)
    got.exchange([
        (u1, whole(same(-1), rel(-1))), (d1, whole(same(1), rel(-1))),
        (u2, whole(same(-1), rel(-2))), (d2, whole(same(1), rel(-2))),
        (z3, whole(same(0), rel(-3))), (z4, half(same(0))), (f1, whole(same(2), rel(-1))),
    ])
    f4 = routes.along_z(half_of(core, f3))
    got.exchange([
        (u3, whole(same(-1), rel(-3))), (d3, whole(same(1), rel(-3))),
        (f2, whole(same(2), rel(-2))), (f3, whole(same(2), rel(-3))),
    ])
    got.exchange([(u4, half(same(-1))), (d4, half(same(1))), (f4, half(same(2)))])
    return got.whole, early


def state_weights(routes, core, starts, decay_rate, shard_at, rows, zs, most):
    count = most // rows
    half = count // 2
    z = shard_at % zs
    k = jnp.arange(half + 1, dtype=jnp.int32)
    steps = jnp.where(core == 0, k, count - k)
    wrapped = jnp.where(core == 0, z < k, z + k >= zs)
    mine = jnp.where(core == 0, ~wrapped, wrapped) & (k > 0)
    counted = jnp.where(core == 0, True, (k > 0) & (k < half))
    ahead = jnp.where(k == 0, count, steps)
    at = jnp.stack([jnp.full_like(k, shard_at), jnp.full_like(k, shard_at + zs)])
    lo, hi = (at - ahead + 1) * rows, at * rows
    broken = jnp.any((starts >= lo[..., None]) & (starts < hi[..., None]), axis=2)
    used = jnp.stack([mine, ~mine]) & counted & ~broken
    both = joined(core, decay_rate[None], routes.swap(decay_rate)[None], 0)
    away = ((ahead - 1) * rows).astype(F32)
    return used.astype(F32)[:, :, None, None, None] * jnp.exp(-both[None] * away[:, None, None, None])[None]


def entering_state(routes, core, last, fq, weights):
    going = joined(core, last[None], routes.swap(last)[None], 0)
    sums = weights[:, 0] * going
    for k in range(1, weights.shape[1]):
        going = routes.along_z(going)
        if k == 1:
            going, fq = lax.optimization_barrier((going, fq))
        sums = sums + weights[:, k] * going
    pick = lambda c: lax.dynamic_index_in_dim(sums, c, 1, keepdims=False)
    total = pick(core) + routes.swap(pick(1 - core))
    return total[0] + routes.next_x(total[1]), fq


def sum_over_channels(gated, out_weight, routes, chips, y, core):
    rows = gated.shape[0]
    width = out_weight.shape[1] // (2 * chips)
    way = 1 - 2 * core
    halves = [gated[: rows // 2], gated[rows // 2 :]]
    dot = lambda a, b: jnp.dot(a, b, preferred_element_type=F32)
    totals = [None, None]
    for k in range(chips - 1, -1, -1):
        mine = lax.dynamic_slice_in_dim(out_weight, (2 * ((y + k * way) % chips) + core) * width, width, axis=1)
        other = lax.dynamic_slice_in_dim(out_weight, (2 * ((y - k * way) % chips) + 1 - core) * width, width, axis=1)
        for i, part in enumerate(halves):
            if totals[i] is not None:
                part, _ = lax.optimization_barrier((part, totals[i]))
            block = lax.optimization_barrier(dot(part, mine)) + routes.swap(dot(part, other).astype(BF16)).astype(F32)
            if totals[i] is not None:
                block = block + routes.along_y(totals[i]).astype(F32)
            totals[i] = block.astype(BF16)
    return jnp.concatenate(totals, 0)


def per_device(xs, zs, tokens, in_weight, short_weight, decay_rate, residue, out_weight, contig_lengths):
    rows, width = tokens.shape
    chans = in_weight.shape[2]
    shards, chips = lax.axis_size("seq"), lax.axis_size("ch") // 2
    shard_at, place_ch = lax.axis_index("seq"), lax.axis_index("ch")
    y, core = place_ch // 2, place_ch % 2
    block = 2 * LANES
    most = 6144
    routes = Routes(chips, xs, zs)
    place = jnp.stack([shard_at // zs, shard_at % zs, core]).astype(jnp.int32)

    grouped = in_weight.reshape(-1, 3, chans // block, block)
    kv = jnp.concatenate([grouped[:, 1], grouped[:, 2]], axis=2).reshape(-1, 2 * chans)
    own = jnp.concatenate([kv, in_weight[:, 0]], axis=1)
    starts, *masks = flags(contig_lengths, shard_at, rows)
    coef = residue * jnp.sqrt(-jnp.expm1(-2.0 * decay_rate))
    d = jnp.exp(-decay_rate)
    d_chunk = jnp.exp(-decay_rate * (rows // CHUNKS))
    weights = state_weights(routes, core, starts, decay_rate, shard_at, rows, zs, most)
    early = (tokens[rows - HALO :], tokens, *masks, jnp.stack([d, d_chunk, coef]), weights)
    whole, early = gather_rows_first(routes, core, place, own, early)
    padded, keep, mask2, keep_s, tail, thru, rates, weights = early
    kw, vw, qw = short_weight[1], short_weight[2], short_weight[0]
    drive, ends, last = call_drive(padded, whole, kw, vw, keep, mask2, tail, thru, rates, block)
    fq = call_query(padded, whole, qw, keep, mask2)
    enter, fq = entering_state(routes, core, last, fq, weights)
    gated = call_gate(drive, ends, enter, fq, keep_s, thru, block)

    return sum_over_channels(gated, out_weight, routes, chips, y, core)


def solution(mesh):
    placed = (
        P("seq", None),
        P("seq", None, "ch"),
        P(None, None, "ch"),
        P(None, "ch"),
        P(None, "ch"),
        P("ch", None),
        P(),
    )
    return jax.shard_map(
        functools.partial(per_device, 4, 8), mesh=mesh, in_specs=placed, out_specs=P("seq", "ch"), check_vma=False
    )
```
